128 devices in a mesh: pipe: 2 (over core), tensor: 4 (over x), dp: 16 (over z, y).
Axes of the slice: x: 4, y: 4, z: 4, core: 2. Of those that a mesh axis runs over, the one named last changes fastest.
Arguments:
- x_saved: bfloat16 [2, 16, 2, 256, 4096], P('pipe', 'dp', None, 'tensor'), may hold values from -6 to 6
- grad_top: bfloat16 [2, 16, 256, 4096], P('pipe', 'dp', 'tensor'), may hold values from -6 to 6
- query: bfloat16 [2, 16, 2, 256, 4096], P('pipe', 'dp', None, None, 'tensor'), may hold values from -16 to 16
- key: bfloat16 [2, 16, 2, 256, 1024], P('pipe', 'dp', None, None, 'tensor'), may hold values from -16 to 16
- value: bfloat16 [2, 16, 2, 256, 1024], P('pipe', 'dp', None, None, 'tensor'), may hold values from -6 to 6
- segment: int32 [2, 16, 2, 256], P('pipe', 'dp'), may hold values from 0 to 3, never falling along the last dimension, each value on 1 to 128 neighbouring positions
- w_query: bfloat16 [2, 4096, 4096], P('pipe', 'dp', 'tensor'), may hold values from -0.09375 to 0.09375
- key_weight: bfloat16 [2, 4096, 1024], P('pipe', 'dp', 'tensor'), may hold values from -0.09375 to 0.09375
- value_weight: bfloat16 [2, 4096, 1024], P('pipe', 'dp', 'tensor'), may hold values from -0.09375 to 0.09375
- w_out: bfloat16 [2, 4096, 4096], P('pipe', 'dp', 'tensor'), may hold values from -0.09375 to 0.09375
- gain: float32 [2, 4096], P('pipe'), may hold values from 0.1 to 1.9
Outputs:
- grad_bottom: bfloat16 [2, 16, 256, 4096], P('pipe', 'dp', 'tensor')
- grad_query: bfloat16 [2, 4096, 4096], P('pipe', 'dp', 'tensor')
- grad_key: bfloat16 [2, 4096, 1024], P('pipe', 'dp', 'tensor')
- grad_value: bfloat16 [2, 4096, 1024], P('pipe', 'dp', 'tensor')
- grad_out: bfloat16 [2, 4096, 4096], P('pipe', 'dp', 'tensor')
- grad_gain: float32 [2, 4096], P('pipe')
The draws below stay inside these ranges and needn't reach their ends.
Inputs may be any that keep to these rules, and one draw needn't show every extreme that they name: `segment`: document ids never fall along a micro-batch.
All inputs are finite; a program needn't handle non-finite values.
Results may differ from the reference program's by a relative error of at most 0.029.
Values may be sent and summed in bfloat16 or wider, within the bound.
A program may use at most 384 MiB of HBM per device.

```python
import math
import jax
import jax.numpy as jnp
import numpy as np
from jax import lax

MODEL_WIDTH = 4096
QUERY_HEADS = 32
KEY_VALUE_HEADS = 8
HEAD_SIZE = 128
MICRO_TOKENS = 256
RELAY_SECTIONS = 2
DATA_REPLICAS = 16


def draw_query(key, part):
    own_key = jax.random.fold_in(key, 11)
    query_group_width = QUERY_HEADS // KEY_VALUE_HEADS
    complete_shape = (RELAY_SECTIONS, DATA_REPLICAS, 2, MICRO_TOKENS, KEY_VALUE_HEADS, query_group_width, HEAD_SIZE)
    start_offset = jnp.clip(jax.random.normal(own_key, complete_shape, jnp.float32), -4.0, 4.0)
    return start_offset.reshape(RELAY_SECTIONS, DATA_REPLICAS, 2, MICRO_TOKENS, QUERY_HEADS * HEAD_SIZE).astype(jnp.bfloat16)


def draw_key(key, part):
    own_key = jax.random.fold_in(key, 12)
    complete_shape = (RELAY_SECTIONS, DATA_REPLICAS, 2, MICRO_TOKENS, KEY_VALUE_HEADS, HEAD_SIZE)
    start_offset = jnp.clip(jax.random.normal(own_key, complete_shape, jnp.float32), -4.0, 4.0)
    return start_offset.reshape(RELAY_SECTIONS, DATA_REPLICAS, 2, MICRO_TOKENS, KEY_VALUE_HEADS * HEAD_SIZE).astype(jnp.bfloat16)


def levels(rng, shape, split, low, largest):
    loudness = 1.0
    for axis_at, shards_of in split:
        draws = jax.random.uniform(jax.random.fold_in(jax.random.fold_in(rng, 6), axis_at), (shards_of,), jnp.float32, low / len(split), largest / len(split))
        loudness = loudness * jnp.repeat(jnp.exp(draws), shape[axis_at] // shards_of).reshape((-1,) + (1,) * (len(shape) - 1 - axis_at))
    return loudness


def profile(number_of, total, reach, slope):
    loads = [(1 << 20) // math.isqrt(rank ** slope) + 1 for rank in range(2, number_of + 1)]
    rest, holding = total - reach - (number_of - 1), [1] * (number_of - 1)
    while rest > 0:
        movable = [i for i in range(number_of - 1) if holding[i] < reach]
        pool, budget = sum([loads[i] for i in movable]), rest
        for i in movable:
            addition = min(reach - holding[i], max(1, budget * loads[i] // pool), rest)
            holding[i] = holding[i] + addition
            rest = rest - addition
    return np.array([reach] + holding)


def ragged(rng, amount, total, bound, lean):
    if amount == 2:
        one = jax.random.randint(rng, (), max(1, total - bound), min(bound, total - 1) + 1)
        return jnp.stack([one, total - one])
    tallies = jnp.asarray(profile(amount, total, bound, lean), jnp.int32)
    couples = (amount - 1) // 2
    donor, receiver = tallies[1:1 + 2 * couples:2], tallies[2:2 + 2 * couples:2]
    room = jnp.minimum(donor - 1, bound - receiver)
    moved = jax.random.randint(jax.random.fold_in(rng, 1), (couples,), 0, 1 << 20) % (room + 1)
    tallies = tallies.at[1:1 + 2 * couples:2].set(donor - moved).at[2:2 + 2 * couples:2].set(receiver + moved)
    return tallies[jax.random.permutation(jax.random.fold_in(rng, 2), amount)]


def noise(key, shape, width, reach, shards=(), held_as=jnp.bfloat16):
    values = width * jax.random.normal(key, shape, jnp.float32)
    if shards:
        values = values * levels(key, shape, shards, -0.22, 0.18)
    return jnp.clip(values, -reach, reach).astype(held_as)


def setup_inputs(seed: int = 0) -> dict:
    splits = jax.random.split(jax.random.key(seed), 12)
    return {
        "x_saved": noise(splits[0], (RELAY_SECTIONS, DATA_REPLICAS, 2, MICRO_TOKENS, MODEL_WIDTH), 1.0, 6.0, ((0, 2), (1, 16), (3, 4))),
        "grad_top": noise(splits[1], (RELAY_SECTIONS, DATA_REPLICAS, MICRO_TOKENS, MODEL_WIDTH), 1.0, 6.0, ((0, 2), (1, 16), (2, 4))),
        "query": draw_query(jax.random.fold_in(splits[11], 71), 0),
        "key": draw_key(jax.random.fold_in(splits[11], 71), 0),
        "value": noise(splits[4], (RELAY_SECTIONS, DATA_REPLICAS, 2, MICRO_TOKENS, KEY_VALUE_HEADS * HEAD_SIZE), 1.0, 6.0, ((0, 2), (1, 16), (4, 4))),
        "segment": jax.vmap(lambda own: jnp.searchsorted(jnp.cumsum(ragged(own, 4, MICRO_TOKENS, MICRO_TOKENS // 2, 0)), jnp.arange(MICRO_TOKENS), side="right"))(jax.random.split(splits[5], RELAY_SECTIONS * DATA_REPLICAS * 2)).reshape((RELAY_SECTIONS, DATA_REPLICAS, 2, MICRO_TOKENS)).astype(jnp.int32),
        "w_query": noise(splits[6], (RELAY_SECTIONS, MODEL_WIDTH, QUERY_HEADS * HEAD_SIZE), MODEL_WIDTH ** -0.5, 0.09375, ((0, 2), (1, 16), (2, 4))),
        "key_weight": noise(splits[7], (RELAY_SECTIONS, MODEL_WIDTH, KEY_VALUE_HEADS * HEAD_SIZE), MODEL_WIDTH ** -0.5, 0.09375, ((0, 2), (1, 16), (2, 4))),
        "value_weight": noise(splits[8], (RELAY_SECTIONS, MODEL_WIDTH, KEY_VALUE_HEADS * HEAD_SIZE), MODEL_WIDTH ** -0.5, 0.09375, ((0, 2), (1, 16), (2, 4))),
        "w_out": noise(splits[9], (RELAY_SECTIONS, MODEL_WIDTH, QUERY_HEADS * HEAD_SIZE), (QUERY_HEADS * HEAD_SIZE) ** -0.5, 0.09375, ((0, 2), (1, 16), (2, 4))),
        "gain": jnp.clip(1.0 + 0.18 * jax.random.normal(splits[10], (RELAY_SECTIONS, MODEL_WIDTH), jnp.float32), 0.1, 1.9),
    }


NORM_EPSILON = 1e-05

def rounded(values):
    return lax.optimization_barrier(values.astype(jnp.bfloat16)).astype(jnp.float32)

def layer_backward(saved_rows, upstream, query_row_block, key_row_block, value_row_block, segment_ids, full_query, full_key, full_value, full_out, gain_row):
    token_length = query_row_block.shape[0]
    query_group_width = QUERY_HEADS // KEY_VALUE_HEADS
    score_scale = 1.0 / math.sqrt(HEAD_SIZE)
    query_head_split = query_row_block.astype(jnp.float32).reshape(token_length, KEY_VALUE_HEADS, query_group_width, HEAD_SIZE)
    key_head_split = key_row_block.astype(jnp.float32).reshape(token_length, KEY_VALUE_HEADS, HEAD_SIZE)
    value_head_split = value_row_block.astype(jnp.float32).reshape(token_length, KEY_VALUE_HEADS, HEAD_SIZE)
    scores = jnp.einsum('ikgd,jkd->kgij', query_head_split, key_head_split) * score_scale
    row_ids = jnp.arange(token_length, dtype=jnp.int32)[:, None]
    col_ids = jnp.arange(token_length, dtype=jnp.int32)[None, :]
    allowed = (col_ids <= row_ids) & (segment_ids[:, None] == segment_ids[None, :])
    scores = jnp.where(allowed, scores, -jnp.inf)
    attention = jax.nn.softmax(scores, axis=-1)
    attention_second = rounded(attention)
    attended = jnp.einsum('kgij,jkd->ikgd', attention_second, value_head_split).astype(jnp.bfloat16).reshape(token_length, QUERY_HEADS * HEAD_SIZE)
    x_float = saved_rows.astype(jnp.float32)
    inv_rms = lax.rsqrt(lax.optimization_barrier(jnp.mean(x_float * x_float, axis=-1, keepdims=True)) + NORM_EPSILON)
    unit_rows = x_float * inv_rms
    normed = (unit_rows * gain_row).astype(jnp.bfloat16)
    attention_gradient = rounded(jnp.dot(upstream, full_out, preferred_element_type=jnp.float32))
    head_gradient = attention_gradient.reshape(token_length, KEY_VALUE_HEADS, query_group_width, HEAD_SIZE)
    grad_probs = jnp.einsum('ikgd,jkd->kgij', head_gradient, value_head_split)
    row_dot = lax.optimization_barrier(jnp.sum(attention * grad_probs, axis=-1, keepdims=True))
    score_gradient = rounded(attention * (grad_probs - row_dot) * score_scale)
    grad_q = jnp.einsum('kgij,jkd->ikgd', score_gradient, key_head_split).astype(jnp.bfloat16).reshape(token_length, QUERY_HEADS * HEAD_SIZE)
    key_gradient = jnp.einsum('eshv,hest->vet', score_gradient, query_head_split).astype(jnp.bfloat16).reshape(token_length, KEY_VALUE_HEADS * HEAD_SIZE)
    value_gradient = jnp.einsum('eshv,hest->vet', attention_second, head_gradient).astype(jnp.bfloat16).reshape(token_length, KEY_VALUE_HEADS * HEAD_SIZE)
    grad_normed = jnp.dot(grad_q, full_query.T, preferred_element_type=jnp.float32)
    grad_normed = grad_normed + jnp.dot(key_gradient, full_key.T, preferred_element_type=jnp.float32)
    grad_normed = grad_normed + jnp.dot(value_gradient, full_value.T, preferred_element_type=jnp.float32)
    scaled = gain_row * grad_normed
    grad_input = upstream.astype(jnp.float32) + inv_rms * (scaled - unit_rows * lax.optimization_barrier(jnp.mean(unit_rows * scaled, axis=-1, keepdims=True)))
    term_list = (jnp.dot(normed.T, grad_q, preferred_element_type=jnp.float32), jnp.dot(normed.T, key_gradient, preferred_element_type=jnp.float32), jnp.dot(normed.T, value_gradient, preferred_element_type=jnp.float32), jnp.dot(upstream.T, attended, preferred_element_type=jnp.float32), lax.optimization_barrier(jnp.sum(grad_normed * unit_rows, axis=0)))
    return (grad_input.astype(jnp.bfloat16), term_list)

def reference(x_saved, grad_top, query, key, value, segment, w_query, key_weight, value_weight, w_out, gain):
    section_count = x_saved.shape[0]
    replica_count = x_saved.shape[1]

    def one_section(section_index, batch_index, upstream_all):
        totals = None
        results = []
        for replica in range(replica_count):
            grad_input, term_list = layer_backward(x_saved[section_index, replica, batch_index], upstream_all[replica], query[section_index, replica, batch_index], key[section_index, replica, batch_index], value[section_index, replica, batch_index], segment[section_index, replica, batch_index], w_query[section_index], key_weight[section_index], value_weight[section_index], w_out[section_index], gain[section_index])
            if totals is None:
                totals = term_list
            else:
                totals = tuple((a + b for a, b in zip(totals, term_list)))
            results.append(grad_input)
        return (jnp.stack(results), totals)

    def first_step(section_index):
        return one_section(section_index, 0, grad_top[section_index])
    section_ids = jnp.arange(section_count, dtype=jnp.int32)
    first_grad, earlier = lax.map(first_step, section_ids)

    def second_step(item_pair):
        section_index, carried = item_pair
        above = (section_index + 1) % section_count
        grad_rows, totals = one_section(section_index, 1, first_grad[above])
        summed = tuple((a + b for a, b in zip(carried, totals)))
        return (grad_rows, (summed[0].astype(jnp.bfloat16), summed[1].astype(jnp.bfloat16), summed[2].astype(jnp.bfloat16), summed[3].astype(jnp.bfloat16), summed[4]))
    bottom, finals = lax.map(second_step, (section_ids, earlier))
    return (bottom, finals[0], finals[1], finals[2], finals[3], finals[4])
```

```python
import functools
import math

import jax
import jax.numpy as jnp
from jax import lax
from jax.experimental import pallas as pl
from jax.experimental.pallas import tpu as pltpu
from jax.sharding import PartitionSpec as P

BF16 = jnp.bfloat16
F32 = jnp.float32
MESH = pl.DeviceIdType.MESH
HEAD = 128
EPS = 1e-05
RING = 4
TOK = 256
SUB = 64
WIDTH = 4096
GROUP = 1024
BLOCK = 256
QCOLS = 1024
KVCOLS = 256
DCOLS = QCOLS + 2 * KVCOLS
ALLCOLS = DCOLS + QCOLS
SCALE = 1.0 / math.sqrt(HEAD)
ORDER = (1, 3, 2)


def nn(left, right):
    return lax.dot_general(left, right, (((1,), (0,)), ((), ())), preferred_element_type=F32)


def nt(left, right):
    return lax.dot_general(left, right, (((1,), (1,)), ((), ())), preferred_element_type=F32)


def tn(left, right):
    return lax.dot_general(left, right, (((0,), (0,)), ((), ())), preferred_element_type=F32)


def at(index, size):
    return pl.ds(pl.multiple_of(index * size, size), size)


def kernel(
    x_ref, top_ref, q_ref, k_ref, v_ref, seg_ref, gain_ref, wq_ref, wk_ref, wv_ref, wo_ref,
    bottom_ref, gq_ref, gk_ref, gv_ref, go_ref, gg_ref,
    up_own, nm_own, up_all, nm_all, w_out, w_qkv, d_all, att_all, g_part, g_recv, g_own, probs,
    n_part, n_recv, n_sum, f_recv, pipe_src, p_part, p_recv, inv_ref, gn_own,
    gain_mine, gain_x, gain_a, gain_b,
    send_sem, up_a_sem, up_x_sem, nm_a_sem, nm_x_sem, w_sem, r_sem, d_sem, att_sem, n_sem, f_sem,
    pipe_sem, p_sem, gx_sem, ga_sem, gb_sem, local_sem,
):
    p = lax.axis_index("pipe")
    t = lax.axis_index("tensor")
    dp = lax.axis_index("dp")
    z = lax.div(dp, RING)
    y = lax.rem(dp, RING)
    a = (1 - p) * z + p * y
    b = (1 - p) * y + p * z

    def dp_of(aa, bb):
        return (1 - p) * (RING * aa + bb) + p * (RING * bb + aa)

    def plus(i, o):
        return lax.rem(i + o, RING)

    def dev_x(o):
        return (p, plus(t, o), dp)

    def dev_a(o):
        return (p, t, dp_of(plus(a, o), b))

    def dev_b(o):
        return (p, t, dp_of(a, plus(b, o)))

    dev_p = (1 - p, t, dp)

    sends = []

    def send(src, dst, recv_sem, device):
        copy = pltpu.make_async_remote_copy(
            src_ref=src, dst_ref=dst, send_sem=send_sem.at[len(sends)], recv_sem=recv_sem,
            device_id=device, device_id_type=MESH,
        )
        copy.start()
        sends.append(copy)
        return copy

    def arrived(dst, recv_sem):
        pltpu.make_async_remote_copy(
            src_ref=dst, dst_ref=dst, send_sem=send_sem.at[0], recv_sem=recv_sem,
            device_id=dev_p, device_id_type=MESH,
        ).wait_recv()

    barrier = pltpu.get_barrier_semaphore()
    partners = [f(o) for f in (dev_x, dev_a, dev_b) for o in ORDER] + [dev_p]
    for device in partners:
        pl.semaphore_signal(barrier, inc=1, device_id=device, device_id_type=MESH)

    blocks = [(i, j) for i in range(RING) for j in range(RING)]

    def cols_of(j):
        return pl.ds(j * BLOCK, BLOCK)

    own_weights = [
        pltpu.make_async_copy(wo_ref, w_out.at[at(b, BLOCK), :], local_sem.at[0]),
        pltpu.make_async_copy(wq_ref, w_qkv.at[at(b, BLOCK), pl.ds(0, QCOLS)], local_sem.at[1]),
        pltpu.make_async_copy(
            wk_ref, w_qkv.at[at(b, BLOCK), pl.ds(QCOLS, KVCOLS)], local_sem.at[2]
        ),
        pltpu.make_async_copy(
            wv_ref, w_qkv.at[at(b, BLOCK), pl.ds(QCOLS + KVCOLS, KVCOLS)], local_sem.at[3]
        ),
    ]
    for copy in own_weights:
        copy.start()

    for i, j in blocks:
        up_own[0, i, :, cols_of(j)] = top_ref[:, at(dp_of(i, j), BLOCK)]

    pl.semaphore_wait(barrier, len(partners))

    def slab(i):
        return pl.ds(pl.multiple_of(i * TOK + t * SUB, SUB), SUB)

    def spread_a(own, gathered, sem, m):
        for o in ORDER:
            send(own.at[m, plus(a, o)], gathered.at[m, slab(a), :], sem.at[m, a], dev_a(o))
        gathered[m, slab(a), :] = own[m, a]

    def spread_x(gathered, a_sem, sem, m):
        for step in (0,) + ORDER:
            i = plus(a, step)
            if step:
                arrived(gathered.at[m, slab(i), :], a_sem.at[m, i])
            for o in ORDER:
                send(
                    gathered.at[m, slab(i), :], gathered.at[m, slab(i), :], sem.at[m, i, t], dev_x(o)
                )

    def wait_x(gathered, sem, m, i):
        for o in ORDER:
            source = plus(t, o)
            rows = pl.ds(pl.multiple_of(i * TOK + source * SUB, SUB), SUB)
            arrived(gathered.at[m, rows, :], sem.at[m, i, source])

    spread_a(up_own, up_all, up_a_sem, 0)
    for o in ORDER:
        send(wo_ref, w_out.at[at(b, BLOCK), :], w_sem.at[0, b], dev_b(o))
    for o in ORDER:
        send(wq_ref, w_qkv.at[at(b, BLOCK), pl.ds(0, QCOLS)], w_sem.at[1, b], dev_b(o))
        send(wk_ref, w_qkv.at[at(b, BLOCK), pl.ds(QCOLS, KVCOLS)], w_sem.at[2, b], dev_b(o))
        send(wv_ref, w_qkv.at[at(b, BLOCK), pl.ds(QCOLS + KVCOLS, KVCOLS)], w_sem.at[3, b], dev_b(o))

    def norm(m):
        square = jnp.zeros((SUB, 1), F32)
        for f in range(16):
            x = x_ref[m, :, cols_of(f)].astype(F32)
            square = square + jnp.sum(x * x, axis=-1, keepdims=True)
        inv = lax.rsqrt(square * (1.0 / WIDTH) + EPS)
        inv_ref[m] = jnp.broadcast_to(inv, (SUB, HEAD))
        for i, j in blocks:
            feature = at(dp_of(i, j), BLOCK)
            x = x_ref[m, :, feature].astype(F32)
            nm_own[m, i, :, cols_of(j)] = (x * inv * gain_ref[:, feature]).astype(BF16)

    spread_x(up_all, up_a_sem, up_x_sem, 0)
    norm(0)
    norm(1)
    spread_a(nm_own, nm_all, nm_a_sem, 0)
    spread_a(nm_own, nm_all, nm_a_sem, 1)

    rows_own = at(a, TOK)

    def forward(m):
        seg_row = jnp.broadcast_to(seg_ref[m : m + 1, :], (TOK, TOK)).astype(F32)
        seg_col = jnp.transpose(seg_row)
        row = lax.broadcasted_iota(jnp.int32, (TOK, TOK), 0)
        col = lax.broadcasted_iota(jnp.int32, (TOK, TOK), 1)
        allowed = (row <= col) & (seg_row == seg_col)
        bias = jnp.where(allowed, 0.0, -1e30).astype(F32)

        def group(g, carry):
            key = k_ref[m, :, at(g, HEAD)]
            value = v_ref[m, :, at(g, HEAD)]
            for h in range(RING):
                cols = at(g * RING + h, HEAD)
                scores = nt(key, q_ref[m, :, cols]) * SCALE + bias
                top = jnp.max(scores, axis=0, keepdims=True)
                raised = jnp.exp(scores - top)
                attention = raised * (1.0 / jnp.sum(raised, axis=0, keepdims=True))
                probs[m, g * RING + h] = attention
                att_all[m, rows_own, cols] = tn(attention.astype(BF16), value).astype(BF16)
            return carry

        lax.fori_loop(0, 2, group, 0)

    def grad_attn_partial(m):
        def rows(i, dst):
            def chunk(n, carry):
                cols = at(n, BLOCK)
                dst[:, cols] = nn(up_all[m, at(i, TOK), :], w_out[:, cols]).astype(BF16)
                return carry

            lax.fori_loop(0, RING, chunk, 0)

        for o in ORDER:
            i = plus(a, o)
            wait_x(up_all, up_x_sem, m, i)
            rows(i, g_part.at[i])
            send(g_part.at[i], g_recv.at[m, a], r_sem.at[m, a], dev_a(o))
        wait_x(up_all, up_x_sem, m, a)
        rows(a, g_recv.at[m, a])

    def grad_attn_sum(m):
        for o in ORDER:
            arrived(g_recv.at[m, plus(a, o)], r_sem.at[m, plus(a, o)])
        for n in range(RING):
            cols = cols_of(n)
            total = g_recv[m, 0, :, cols].astype(F32)
            for i in range(1, RING):
                total = total + g_recv[m, i, :, cols].astype(F32)
            g_own[:, cols] = total.astype(BF16)

    def backward(m):
        def group(g, carry):
            key = k_ref[m, :, at(g, HEAD)]
            value = v_ref[m, :, at(g, HEAD)]
            dk = jnp.zeros((TOK, HEAD), F32)
            dv = jnp.zeros((TOK, HEAD), F32)
            for h in range(RING):
                cols = at(g * RING + h, HEAD)
                grad = g_own[:, cols]
                attention = probs[m, g * RING + h]
                grad_probs = nt(value, grad)
                row_dot = jnp.sum(attention * grad_probs, axis=0, keepdims=True)
                score = (attention * (grad_probs - row_dot) * SCALE).astype(BF16)
                d_all[m, rows_own, cols] = tn(score, key).astype(BF16)
                dk = dk + nn(score, q_ref[m, :, cols])
                dv = dv + nn(attention.astype(BF16), grad)
            d_all[m, rows_own, pl.ds(pl.multiple_of(QCOLS + g * HEAD, HEAD), HEAD)] = dk.astype(BF16)
            d_all[m, rows_own, pl.ds(pl.multiple_of(QCOLS + KVCOLS + g * HEAD, HEAD), HEAD)] = (
                dv.astype(BF16)
            )
            return carry

        lax.fori_loop(0, 2, group, 0)

    def spread_d(m):
        for o in ORDER:
            send(d_all.at[m, rows_own, :], d_all.at[m, rows_own, :], d_sem.at[m, a], dev_a(o))
        for o in ORDER:
            send(att_all.at[m, rows_own, :], att_all.at[m, rows_own, :], att_sem.at[m, a], dev_a(o))

    def grad_normed_partial(m):
        for step in (0,) + ORDER:
            i = plus(a, step)
            if step:
                arrived(d_all.at[m, at(i, TOK), :], d_sem.at[m, i])

            def chunk(n, carry):
                cols = at(n, BLOCK)
                part = nt(d_all[m, at(i, TOK), :], w_qkv[at(n, BLOCK), :]).astype(BF16)
                for u in range(RING):
                    n_part[u, i, :, cols] = part[u * SUB : (u + 1) * SUB, :]
                return carry

            lax.fori_loop(0, RING, chunk, 0)
            for o in ORDER:
                send(
                    n_part.at[plus(t, o), i], n_recv.at[m, t, i], n_sem.at[m, t, i], dev_x(o)
                )
            n_recv[m, t, i] = n_part[t, i]

    def grad_normed_sum(m):
        for step in ORDER + (0,):
            i = plus(a, step)
            for o in ORDER:
                arrived(n_recv.at[m, plus(t, o), i], n_sem.at[m, plus(t, o), i])
            for n in range(RING):
                cols = cols_of(n)
                total = n_recv[m, 0, i, :, cols].astype(F32)
                for u in range(1, RING):
                    total = total + n_recv[m, u, i, :, cols].astype(F32)
                n_sum[i, :, cols] = total.astype(BF16)
            if step:
                send(n_sum.at[i], f_recv.at[m, a], f_sem.at[m, a], dev_a(step))
        f_recv[m, a] = n_sum[a]
        for o in ORDER:
            arrived(f_recv.at[m, plus(a, o)], f_sem.at[m, plus(a, o)])

    def grad_input(m):
        inv = inv_ref[m][:, :1]
        total = jnp.zeros((SUB, 1), F32)
        for i, j in blocks:
            feature = at(dp_of(i, j), BLOCK)
            unit = x_ref[m, :, feature].astype(F32) * inv
            grad = f_recv[m, i, :, cols_of(j)].astype(F32)
            term = unit * grad
            total = total + jnp.sum(term * gain_ref[:, feature], axis=-1, keepdims=True)
            place = (pl.ds(i * 2 + j // 2, 1), cols_of(j % 2))
            gain_sum = jnp.sum(term, axis=0, keepdims=True)
            if m == 0:
                gain_mine[place] = gain_sum
            else:
                gain_mine[place] = gain_mine[place] + gain_sum
        mean = total * (1.0 / WIDTH)
        for i, j in blocks:
            feature = at(dp_of(i, j), BLOCK)
            unit = x_ref[m, :, feature].astype(F32) * inv
            grad = f_recv[m, i, :, cols_of(j)].astype(F32)
            result = up_own[m, i, :, cols_of(j)].astype(F32) + inv * (
                gain_ref[:, feature] * grad - unit * mean
            )
            if m == 0:
                pipe_src[i, :, cols_of(j)] = result.astype(BF16)
            else:
                bottom_ref[:, feature] = result.astype(BF16)

    forward(0)
    own_weights[0].wait()
    for o in ORDER:
        arrived(w_out.at[at(plus(b, o), BLOCK), :], w_sem.at[0, plus(b, o)])
    grad_attn_partial(0)
    spread_x(nm_all, nm_a_sem, nm_x_sem, 0)
    forward(1)
    grad_attn_sum(0)
    backward(0)
    spread_d(0)
    for copy in own_weights[1:]:
        copy.wait()
    for o in ORDER:
        rows = at(plus(b, o), BLOCK)
        arrived(w_qkv.at[rows, pl.ds(0, QCOLS)], w_sem.at[1, plus(b, o)])
        arrived(w_qkv.at[rows, pl.ds(QCOLS, KVCOLS)], w_sem.at[2, plus(b, o)])
        arrived(w_qkv.at[rows, pl.ds(QCOLS + KVCOLS, KVCOLS)], w_sem.at[3, plus(b, o)])
    grad_normed_partial(0)
    n_sends = sends[-12:]
    grad_normed_sum(0)
    grad_input(0)
    for i, j in blocks:
        send(
            pipe_src.at[i, :, cols_of(j)], up_own.at[1, j, :, cols_of(i)], pipe_sem.at[0], dev_p
        )
    spread_x(nm_all, nm_a_sem, nm_x_sem, 1)
    waited = []
    for copy in sends:
        copy.wait_send()
    n_done = len(sends)
    arrived(up_own.at[1], pipe_sem.at[0])

    spread_a(up_own, up_all, up_a_sem, 1)
    spread_x(up_all, up_a_sem, up_x_sem, 1)
    grad_attn_partial(1)
    grad_attn_sum(1)
    backward(1)
    spread_d(1)
    grad_normed_partial(1)

    for m in range(2):
        for i in range(RING):
            wait_x(nm_all, nm_x_sem, m, i)
    for m in range(2):
        for o in ORDER:
            if m == 0:
                pass
            arrived(att_all.at[m, at(plus(a, o), TOK), :], att_sem.at[m, plus(a, o)])

    def weight_grads(j, dst):
        feature = at(j, BLOCK)

        def chunk(n, carry):
            cols = at(n, 512)
            total = tn(nm_all[0, :, feature], d_all[0, :, cols])
            total = total + tn(nm_all[1, :, feature], d_all[1, :, cols])
            dst[:, cols] = total.astype(BF16)
            return carry

        lax.fori_loop(0, DCOLS // 512, chunk, 0)

        def chunk_out(n, carry):
            cols = at(n, 512)
            total = tn(up_all[0, :, feature], att_all[0, :, cols])
            total = total + tn(up_all[1, :, feature], att_all[1, :, cols])
            dst[:, pl.ds(pl.multiple_of(DCOLS + n * 512, 512), 512)] = total.astype(BF16)
            return carry

        lax.fori_loop(0, QCOLS // 512, chunk_out, 0)

    for o in ORDER:
        j = plus(b, o)
        weight_grads(j, p_part.at[j])
        send(p_part.at[j], p_recv.at[b], p_sem.at[b], dev_b(o))
    weight_grads(b, p_recv.at[b])

    grad_normed_sum(1)
    grad_input(1)

    gain_x[t] = gain_mine[...]
    for o in ORDER:
        send(gain_x.at[t], gain_x.at[t], gx_sem.at[t], dev_x(o))
    for o in ORDER:
        arrived(gain_x.at[plus(t, o)], gx_sem.at[plus(t, o)])
    gain_a[a] = gain_x[0] + gain_x[1] + gain_x[2] + gain_x[3]
    for o in ORDER:
        send(gain_a.at[a], gain_a.at[a], ga_sem.at[a], dev_a(o))
    for o in ORDER:
        arrived(gain_a.at[plus(a, o)], ga_sem.at[plus(a, o)])
    gain_b[b] = gain_a[0] + gain_a[1] + gain_a[2] + gain_a[3]
    for o in ORDER:
        send(gain_b.at[b], gain_b.at[b], gb_sem.at[b], dev_b(o))
    for o in ORDER:
        arrived(gain_b.at[plus(b, o)], gb_sem.at[plus(b, o)])
    gain_mine[...] = gain_b[0] + gain_b[1] + gain_b[2] + gain_b[3]
    for i, j in blocks:
        gg_ref[:, at(dp_of(i, j), BLOCK)] = gain_mine[pl.ds(i * 2 + j // 2, 1), cols_of(j % 2)]

    for o in ORDER:
        arrived(p_recv.at[plus(b, o)], p_sem.at[plus(b, o)])

    def summed(cols):
        total = p_recv[0, :, cols].astype(F32)
        for i in range(1, RING):
            total = total + p_recv[i, :, cols].astype(F32)
        return total.astype(BF16)

    for n in range(4):
        gq_ref[:, cols_of(n)] = summed(cols_of(n))
        go_ref[:, cols_of(n)] = summed(pl.ds(DCOLS + n * BLOCK, BLOCK))
    gk_ref[...] = summed(pl.ds(QCOLS, KVCOLS))
    gv_ref[...] = summed(pl.ds(QCOLS + KVCOLS, KVCOLS))
    for copy in sends[n_done:]:
        copy.wait_send()


def local(x_saved, grad_top, query, key, value, segment, w_query, key_weight, value_weight, w_out, gain):
    vmem = pl.BlockSpec(memory_space=pltpu.VMEM)
    hbm = pl.BlockSpec(memory_space=pl.ANY)
    dma = pltpu.SemaphoreType.DMA
    outs = pl.pallas_call(
        kernel,
        out_shape=(
            jax.ShapeDtypeStruct((SUB, WIDTH), BF16),
            jax.ShapeDtypeStruct((BLOCK, QCOLS), BF16),
            jax.ShapeDtypeStruct((BLOCK, KVCOLS), BF16),
            jax.ShapeDtypeStruct((BLOCK, KVCOLS), BF16),
            jax.ShapeDtypeStruct((BLOCK, QCOLS), BF16),
            jax.ShapeDtypeStruct((1, WIDTH), F32),
        ),
        in_specs=[vmem] * 7 + [hbm] * 4,
        out_specs=(vmem,) * 6,
        scratch_shapes=[
            pltpu.VMEM((2, RING, SUB, GROUP), BF16),
            pltpu.VMEM((2, RING, SUB, GROUP), BF16),
            pltpu.VMEM((2, GROUP, GROUP), BF16),
            pltpu.VMEM((2, GROUP, GROUP), BF16),
            pltpu.VMEM((GROUP, QCOLS), BF16),
            pltpu.VMEM((GROUP, DCOLS), BF16),
            pltpu.VMEM((2, GROUP, DCOLS), BF16),
            pltpu.VMEM((2, GROUP, QCOLS), BF16),
            pltpu.VMEM((RING, TOK, QCOLS), BF16),
            pltpu.VMEM((2, RING, TOK, QCOLS), BF16),
            pltpu.VMEM((TOK, QCOLS), BF16),
            pltpu.VMEM((2, 8, TOK, TOK), F32),
            pltpu.VMEM((RING, RING, SUB, GROUP), BF16),
            pltpu.VMEM((2, RING, RING, SUB, GROUP), BF16),
            pltpu.VMEM((RING, SUB, GROUP), BF16),
            pltpu.VMEM((2, RING, SUB, GROUP), BF16),
            pltpu.VMEM((RING, SUB, GROUP), BF16),
            pltpu.VMEM((RING, BLOCK, ALLCOLS), BF16),
            pltpu.VMEM((RING, BLOCK, ALLCOLS), BF16),
            pltpu.VMEM((2, SUB, HEAD), F32),
            pltpu.VMEM((8, 128), F32),
            pltpu.VMEM((8, 512), F32),
            pltpu.VMEM((RING, 8, 512), F32),
            pltpu.VMEM((RING, 8, 512), F32),
            pltpu.VMEM((RING, 8, 512), F32),
            dma((200,)),
            dma((2, RING)),
            dma((2, RING, RING)),
            dma((2, RING)),
            dma((2, RING, RING)),
            dma((RING, RING)),
            dma((2, RING)),
            dma((2, RING)),
            dma((2, RING)),
            dma((2, RING, RING)),
            dma((2, RING)),
            dma((1,)),
            dma((RING,)),
            dma((RING,)),
            dma((RING,)),
            dma((RING,)),
            dma((4,)),
        ],
        compiler_params=pltpu.CompilerParams(
            collective_id=0, has_side_effects=True, vmem_limit_bytes=63 * 2**20
        ),
        cost_estimate=pl.CostEstimate(flops=23 * 10**9, bytes_accessed=8 * 10**6, transcendentals=10**6),
        name="relay_backward",
    )(
        x_saved[0, 0], grad_top[0, 0], query[0, 0], key[0, 0], value[0, 0], segment[0, 0], gain,
        w_query[0], key_weight[0], value_weight[0], w_out[0],
    )
    bottom, gq, gk, gv, go, gg = outs
    return (bottom[None, None], gq[None], gk[None], gv[None], go[None], gg)


def solution(mesh):
    in_specs = (
        P("pipe", "dp", None, "tensor", None),
        P("pipe", "dp", "tensor", None),
        P("pipe", "dp", None, None, "tensor"),
        P("pipe", "dp", None, None, "tensor"),
        P("pipe", "dp", None, None, "tensor"),
        P("pipe", "dp", None, None),
        P("pipe", "dp", "tensor"),
        P("pipe", "dp", "tensor"),
        P("pipe", "dp", "tensor"),
        P("pipe", "dp", "tensor"),
        P("pipe", None),
    )
    out_specs = (
        P("pipe", "dp", "tensor", None),
        P("pipe", "dp", "tensor"),
        P("pipe", "dp", "tensor"),
        P("pipe", "dp", "tensor"),
        P("pipe", "dp", "tensor"),
        P("pipe", None),
    )
    return jax.shard_map(local, mesh=mesh, in_specs=in_specs, out_specs=out_specs, check_vma=False)
```

```python
import functools
import math

import jax
import jax.numpy as jnp
from jax import lax
from jax.experimental import pallas as pl
from jax.experimental.pallas import tpu as pltpu
from jax.sharding import PartitionSpec as P

BF16 = jnp.bfloat16
F32 = jnp.float32
MESH = pl.DeviceIdType.MESH
HEAD = 128
EPS = 1e-05
RING = 4
TOK = 256
SUB = 64
WIDTH = 4096
GROUP = 1024
BLOCK = 256
QCOLS = 1024
KVCOLS = 256
DCOLS = QCOLS + 2 * KVCOLS
ALLCOLS = DCOLS + QCOLS
SCALE = 1.0 / math.sqrt(HEAD)
ORDER = (1, 3, 2)


def nn(left, right):
    return lax.dot_general(left, right, (((1,), (0,)), ((), ())), preferred_element_type=F32)


def nt(left, right):
    return lax.dot_general(left, right, (((1,), (1,)), ((), ())), preferred_element_type=F32)


def tn(left, right):
    return lax.dot_general(left, right, (((0,), (0,)), ((), ())), preferred_element_type=F32)


def at(index, size):
    return pl.ds(pl.multiple_of(index * size, size), size)


def kernel(
    x_hbm, top_hbm, q_hbm, k_hbm, v_hbm, seg_ref, gain_ref, wq_ref, wk_ref, wv_ref, wo_ref,
    bottom_ref, gq_ref, gk_ref, gv_ref, go_ref, gg_ref,
    x_ref, q_ref, k_ref, v_ref,
    up_own, nm_own, up_all, nm_all, w_out, w_qkv, d_all, att_all,
    g_part, g_relay, g_recv, g_own, probs,
    n_part, n_relay, n_recv, n_sum, f_recv, pipe_src, p_part, p_relay, p_recv, inv_ref,
    gain_mine, gain_x, gain_a, gain_b,
    send_sem, up_a_sem, up_x_sem, nm_a_sem, nm_x_sem, w_sem, gr_sem, g_sem, d_sem, att_sem,
    nr_sem, n_sem, f_sem, pipe_sem, pr_sem, p_sem, gx_sem, ga_sem, gb_sem, local_sem,
):
    p = lax.axis_index("pipe")
    t = lax.axis_index("tensor")
    dp = lax.axis_index("dp")
    z = lax.div(dp, RING)
    y = lax.rem(dp, RING)
    a = (1 - p) * z + p * y
    b = (1 - p) * y + p * z

    def dp_of(aa, bb):
        return (1 - p) * (RING * aa + bb) + p * (RING * bb + aa)

    def plus(i, o):
        return lax.rem(i + o, RING)

    def dev_x(o):
        return (p, plus(t, o), dp)

    def dev_a(o):
        return (p, t, dp_of(plus(a, o), b))

    def dev_b(o):
        return (p, t, dp_of(a, plus(b, o)))

    dev_p = (1 - p, t, dp)

    sends = []
    unfinished = {}

    def send(src, dst, recv_sem, device):
        copy = pltpu.make_async_remote_copy(
            src_ref=src, dst_ref=dst, send_sem=send_sem.at[len(sends)], recv_sem=recv_sem,
            device_id=device, device_id_type=MESH,
        )
        copy.start()
        sends.append(copy)
        unfinished[id(copy)] = copy
        return copy

    def finish(copies):
        for copy in copies:
            copy.wait_send()
            del unfinished[id(copy)]

    def arrived(dst, recv_sem):
        pltpu.make_async_remote_copy(
            src_ref=dst, dst_ref=dst, send_sem=send_sem.at[0], recv_sem=recv_sem,
            device_id=dev_p, device_id_type=MESH,
        ).wait_recv()

    class Gather:
        def __init__(self, view, sem, me, device):
            self.view, self.sem, self.me, self.device = view, sem, me, device

        def copy(self, owner, half, way):
            place = self.view(owner, half)
            send(place, place, self.sem(owner, half), self.device(way))

        def wait(self, owner, half):
            arrived(self.view(owner, half), self.sem(owner, half))

        def start(self):
            for half, way in ((0, 1), (1, 3), (1, 1), (0, 3)):
                self.copy(self.me, half, way)

        def forward(self):
            for half, origin, way in ((0, 3, 1), (1, 1, 3)):
                owner = plus(self.me, origin)
                self.wait(owner, half)
                self.copy(owner, half, way)

        def near(self):
            self.wait(plus(self.me, 3), 1)
            self.wait(plus(self.me, 1), 0)

        def far(self):
            self.wait(plus(self.me, 2), 0)
            self.wait(plus(self.me, 2), 1)

    class Scatter:
        def __init__(self, part, relay, recv, relay_sem, sem, me, device):
            self.part, self.relay, self.recv = part, relay, recv
            self.relay_sem, self.sem, self.me, self.device = relay_sem, sem, me, device
            self.copies = []

        def far(self):
            for half, way in ((0, 1), (1, 3)):
                self.copies.append(
                    send(self.part(plus(self.me, 2), half), self.relay(half), self.relay_sem(half),
                         self.device(way))
                )

        def direct(self, half):
            way, other = ((1, 3)[half], 1 - half)
            self.copies.append(
                send(self.part(plus(self.me, way), other), self.recv(half, other),
                     self.sem(half, other), self.device(way))
            )

        def onward(self, half):
            way = (1, 3)[half]
            arrived(self.relay(half), self.relay_sem(half))
            place = self.part(plus(self.me, way), half)
            place[...] = (place[...].astype(F32) + self.relay(half)[...].astype(F32)).astype(BF16)
            self.copies.append(
                send(place, self.recv(half, half), self.sem(half, half), self.device(way))
            )

        def wait(self):
            for way in range(2):
                for half in range(2):
                    arrived(self.recv(way, half), self.sem(way, half))

    barrier = pltpu.get_barrier_semaphore()
    partners = [f(o) for f in (dev_x, dev_a, dev_b) for o in ORDER] + [dev_p]
    for device in partners:
        pl.semaphore_signal(barrier, inc=1, device_id=device, device_id_type=MESH)

    blocks = [(i, j) for i in range(RING) for j in range(RING)]

    def cols_of(j):
        return pl.ds(j * BLOCK, BLOCK)

    for i, j in blocks:
        pltpu.make_async_copy(
            top_hbm.at[:, at(dp_of(i, j), BLOCK)], up_own.at[0, i, :, cols_of(j)], local_sem.at[0]
        ).start()
    loads = [
        pltpu.make_async_copy(x_hbm, x_ref, local_sem.at[1]),
        pltpu.make_async_copy(q_hbm, q_ref, local_sem.at[2]),
        pltpu.make_async_copy(k_hbm, k_ref, local_sem.at[3]),
        pltpu.make_async_copy(v_hbm, v_ref, local_sem.at[4]),
        pltpu.make_async_copy(wo_ref, w_out.at[at(b, BLOCK), :], local_sem.at[5]),
        pltpu.make_async_copy(wq_ref, w_qkv.at[at(b, BLOCK), pl.ds(0, QCOLS)], local_sem.at[6]),
        pltpu.make_async_copy(
            wk_ref, w_qkv.at[at(b, BLOCK), pl.ds(QCOLS, KVCOLS)], local_sem.at[7]
        ),
        pltpu.make_async_copy(
            wv_ref, w_qkv.at[at(b, BLOCK), pl.ds(QCOLS + KVCOLS, KVCOLS)], local_sem.at[8]
        ),
    ]
    for copy in loads:
        copy.start()
    pltpu.make_async_copy(up_own.at[0], up_own.at[0], local_sem.at[0]).wait()
    pl.semaphore_wait(barrier, len(partners))

    rows_own = at(a, TOK)

    def half_rows(i, half, size):
        return pl.ds(pl.multiple_of(i * size + half * (size // 2), size // 2), size // 2)

    def slab(i):
        return pl.ds(pl.multiple_of(i * TOK + t * SUB, SUB), SUB)

    def spread_a(own, gathered, sem, m):
        for o in ORDER:
            send(own.at[m, plus(a, o)], gathered.at[m, slab(a), :], sem.at[m, a], dev_a(o))
        gathered[m, slab(a), :] = own[m, a]

    def token_gathers(gathered, sem, m):
        def make(step):
            i = plus(a, step)

            def view(owner, half):
                start = i * TOK + owner * SUB + half * (SUB // 2)
                return gathered.at[m, pl.ds(pl.multiple_of(start, SUB // 2), SUB // 2), :]

            return Gather(view, lambda owner, half: sem.at[m, i, owner, half], t, dev_x)

        return {step: make(step) for step in range(RING)}

    def row_gather(ref, sem, m):
        return Gather(
            lambda owner, half: ref.at[m, half_rows(owner, half, TOK), :],
            lambda owner, half: sem.at[m, owner, half], a, dev_a,
        )

    def weight_gather(ref, cols, index):
        return Gather(
            lambda owner, half: ref.at[half_rows(owner, half, BLOCK), cols],
            lambda owner, half: w_sem.at[index, owner, half], b, dev_b,
        )

    out_gather = weight_gather(w_out, slice(None), 0)
    qkv_gather = weight_gather(w_qkv, slice(None), 1)
    up_gathers = [token_gathers(up_all, up_x_sem, m) for m in range(2)]
    nm_gathers = [token_gathers(nm_all, nm_x_sem, m) for m in range(2)]
    d_gathers = [row_gather(d_all, d_sem, m) for m in range(2)]
    att_gathers = [row_gather(att_all, att_sem, m) for m in range(2)]

    def start_x(gathers, sem, gathered, m):
        for step in (0,) + ORDER:
            i = plus(a, step)
            if step:
                arrived(gathered.at[m, slab(i), :], sem.at[m, i])
            gathers[step].start()

    def norm(m):
        square = jnp.zeros((SUB, 1), F32)
        for f in range(16):
            x = x_ref[m, :, cols_of(f)].astype(F32)
            square = square + jnp.sum(x * x, axis=-1, keepdims=True)
        inv = lax.rsqrt(square * (1.0 / WIDTH) + EPS)
        inv_ref[m] = jnp.broadcast_to(inv, (SUB, HEAD))
        for i, j in blocks:
            feature = at(dp_of(i, j), BLOCK)
            x = x_ref[m, :, feature].astype(F32)
            nm_own[m, i, :, cols_of(j)] = (x * inv * gain_ref[:, feature]).astype(BF16)

    def forward(m):
        seg_row = jnp.broadcast_to(seg_ref[m : m + 1, :], (TOK, TOK)).astype(F32)
        seg_col = jnp.transpose(seg_row)
        row = lax.broadcasted_iota(jnp.int32, (TOK, TOK), 0)
        col = lax.broadcasted_iota(jnp.int32, (TOK, TOK), 1)
        allowed = (row <= col) & (seg_row == seg_col)
        bias = jnp.where(allowed, 0.0, -1e30).astype(F32)

        def group(g, carry):
            key = k_ref[m, :, at(g, HEAD)]
            value = v_ref[m, :, at(g, HEAD)]
            for h in range(RING):
                cols = at(g * RING + h, HEAD)
                scores = nt(key, q_ref[m, :, cols]) * SCALE + bias
                top = jnp.max(scores, axis=0, keepdims=True)
                raised = jnp.exp(scores - top)
                attention = raised * (1.0 / jnp.sum(raised, axis=0, keepdims=True))
                probs[m, g * RING + h] = attention
                att_all[m, rows_own, cols] = tn(attention.astype(BF16), value).astype(BF16)
            return carry

        lax.fori_loop(0, 2, group, 0)

    def grad_attn_rows(m, i, dst):
        def chunk(n, carry):
            cols = at(n, BLOCK)
            dst[:, cols] = nn(up_all[m, at(i, TOK), :], w_out[:, cols]).astype(BF16)
            return carry

        lax.fori_loop(0, RING, chunk, 0)

    def grad_attn_scatter(m):
        return Scatter(
            lambda dest, half: g_part.at[dest, pl.ds(half * 128, 128), :],
            lambda way: g_relay.at[m, way],
            lambda way, half: g_recv.at[m, way, pl.ds(half * 128, 128), :],
            lambda way: gr_sem.at[m, way],
            lambda way, half: g_sem.at[m, way, half],
            a, dev_a,
        )

    def grad_attn_partial(m):
        scatter = grad_attn_scatter(m)
        gathers = up_gathers[m]
        for step in (2, 1, 3, 0):
            gathers[step].near()
            gathers[step].far()
            i = plus(a, step)
            grad_attn_rows(m, i, g_part.at[i])
            if step == 2:
                scatter.far()
            elif step == 1:
                scatter.direct(0)
            elif step == 3:
                scatter.direct(1)
        return scatter

    def grad_attn_sum(m, scatter):
        scatter.onward(0)
        scatter.onward(1)
        scatter.wait()
        for n in range(RING):
            cols = cols_of(n)
            total = g_part[a, :, cols].astype(F32) + g_recv[m, 0, :, cols].astype(F32)
            g_own[:, cols] = (total + g_recv[m, 1, :, cols].astype(F32)).astype(BF16)

    def backward(m):
        def group(g, carry):
            key = k_ref[m, :, at(g, HEAD)]
            value = v_ref[m, :, at(g, HEAD)]
            dk = jnp.zeros((TOK, HEAD), F32)
            dv = jnp.zeros((TOK, HEAD), F32)
            for h in range(RING):
                cols = at(g * RING + h, HEAD)
                grad = g_own[:, cols]
                attention = probs[m, g * RING + h]
                grad_probs = nt(value, grad)
                row_dot = jnp.sum(attention * grad_probs, axis=0, keepdims=True)
                score = (attention * (grad_probs - row_dot) * SCALE).astype(BF16)
                d_all[m, rows_own, cols] = tn(score, key).astype(BF16)
                dk = dk + nn(score, q_ref[m, :, cols])
                dv = dv + nn(attention.astype(BF16), grad)
            d_all[m, rows_own, pl.ds(pl.multiple_of(QCOLS + g * HEAD, HEAD), HEAD)] = dk.astype(BF16)
            d_all[m, rows_own, pl.ds(pl.multiple_of(QCOLS + KVCOLS + g * HEAD, HEAD), HEAD)] = (
                dv.astype(BF16)
            )
            return carry

        lax.fori_loop(0, 2, group, 0)

    def grad_normed_scatter(m, step):
        i = plus(a, step)
        return Scatter(
            lambda dest, half: n_part.at[dest, i, pl.ds(half * 32, 32), :],
            lambda way: n_relay.at[m, way, i],
            lambda way, half: n_recv.at[m, way, i, pl.ds(half * 32, 32), :],
            lambda way: nr_sem.at[m, way, i],
            lambda way, half: n_sem.at[m, way, i, half],
            t, dev_x,
        )

    def grad_normed_rows(m, step):
        i = plus(a, step)

        def chunk(n, carry):
            cols = at(n, BLOCK)
            part = nt(d_all[m, at(i, TOK), :], w_qkv[at(n, BLOCK), :]).astype(BF16)
            for u in range(RING):
                n_part[u, i, :, cols] = part[u * SUB : (u + 1) * SUB, :]
            return carry

        lax.fori_loop(0, RING, chunk, 0)
        scatter = grad_normed_scatter(m, step)
        scatter.far()
        scatter.direct(0)
        scatter.direct(1)
        return scatter

    def onward(scatter):
        scatter.onward(0)
        scatter.onward(1)

    def grad_normed_sum(m, step, scatter):
        i = plus(a, step)
        scatter.wait()
        for n in range(RING):
            cols = cols_of(n)
            total = n_part[t, i, :, cols].astype(F32) + n_recv[m, 0, i, :, cols].astype(F32)
            total = (total + n_recv[m, 1, i, :, cols].astype(F32)).astype(BF16)
            if step:
                n_sum[i, :, cols] = total
            else:
                f_recv[m, i, :, cols] = total
        if step:
            return [send(n_sum.at[i], f_recv.at[m, a], f_sem.at[m, a], dev_a(step))]
        return []

    def grad_normed_back(m):
        for o in ORDER:
            arrived(f_recv.at[m, plus(a, o)], f_sem.at[m, plus(a, o)])

    def grad_input(m):
        inv = inv_ref[m][:, :1]
        total = jnp.zeros((SUB, 1), F32)
        for i, j in blocks:
            feature = at(dp_of(i, j), BLOCK)
            unit = x_ref[m, :, feature].astype(F32) * inv
            grad = f_recv[m, i, :, cols_of(j)].astype(F32)
            term = unit * grad
            total = total + jnp.sum(term * gain_ref[:, feature], axis=-1, keepdims=True)
            place = (pl.ds(i * 2 + j // 2, 1), cols_of(j % 2))
            gain_sum = jnp.sum(term, axis=0, keepdims=True)
            if m == 0:
                gain_mine[place] = gain_sum
            else:
                gain_mine[place] = gain_mine[place] + gain_sum
        mean = total * (1.0 / WIDTH)
        for i, j in blocks:
            feature = at(dp_of(i, j), BLOCK)
            unit = x_ref[m, :, feature].astype(F32) * inv
            grad = f_recv[m, i, :, cols_of(j)].astype(F32)
            result = up_own[m, i, :, cols_of(j)].astype(F32) + inv * (
                gain_ref[:, feature] * grad - unit * mean
            )
            if m == 0:
                pipe_src[i, :, cols_of(j)] = result.astype(BF16)
            else:
                bottom_ref[:, feature] = result.astype(BF16)

    def weight_rows(first, gathered, grads, width, offset):
        def rows(step):
            j = plus(b, step)
            feature = at(j, BLOCK)

            def chunk(n, carry):
                cols = at(n, 512)
                total = tn(gathered[0, :, feature], grads[0, :, cols])
                total = total + tn(gathered[1, :, feature], grads[1, :, cols])
                place = pl.ds(pl.multiple_of(offset + n * 512, 512), 512)
                p_part[j, :, place] = total.astype(BF16)
                return carry

            lax.fori_loop(0, width // 512, chunk, 0)

        scatter = Scatter(
            lambda dest, half: p_part.at[dest, pl.ds(half * 128, 128), pl.ds(offset, width)],
            lambda way: p_relay.at[way, :, pl.ds(offset, width)],
            lambda way, half: p_recv.at[way, pl.ds(half * 128, 128), pl.ds(offset, width)],
            lambda way: pr_sem.at[first, way],
            lambda way, half: p_sem.at[first, way, half],
            b, dev_b,
        )
        rows(2)
        scatter.far()
        rows(1)
        scatter.direct(0)
        rows(3)
        scatter.direct(1)
        rows(0)
        return scatter

    def summed(cols):
        total = p_part[b, :, cols].astype(F32) + p_recv[0, :, cols].astype(F32)
        return (total + p_recv[1, :, cols].astype(F32)).astype(BF16)

    spread_a(up_own, up_all, up_a_sem, 0)
    loads[4].wait()
    out_gather.start()
    up_gathers[0][0].start()
    loads[0].wait()
    norm(0)
    norm(1)
    for step in ORDER:
        i = plus(a, step)
        arrived(up_all.at[0, slab(i), :], up_a_sem.at[0, i])
        up_gathers[0][step].start()
    spread_a(nm_own, nm_all, nm_a_sem, 0)
    spread_a(nm_own, nm_all, nm_a_sem, 1)
    for copy in loads[5:]:
        copy.wait()
    out_gather.forward()
    qkv_gather.start()
    for copy in loads[1:4]:
        copy.wait()
    forward(0)
    for step in (0, 2, 1, 3):
        up_gathers[0][step].forward()
    forward(1)
    att_gathers[0].start()
    out_gather.near()
    out_gather.far()
    scatter = grad_attn_partial(0)
    g_copies = scatter.copies
    qkv_gather.forward()
    start_x(nm_gathers[0], nm_a_sem, nm_all, 0)
    att_gathers[0].forward()
    grad_attn_sum(0, scatter)
    backward(0)
    d_gathers[0].start()
    qkv_gather.near()
    qkv_gather.far()
    for step in range(RING):
        nm_gathers[0][step].forward()
    n_copies = []

    def grad_normed(m):
        scatters = {0: grad_normed_rows(m, 0)}
        d_gathers[m].forward()
        if m == 0:
            att_gathers[1].start()
        d_gathers[m].near()
        onward(scatters[0])
        scatters[1] = grad_normed_rows(m, 1)
        scatters[3] = grad_normed_rows(m, 3)
        onward(scatters[1])
        d_gathers[m].far()
        scatters[2] = grad_normed_rows(m, 2)
        onward(scatters[3])
        return scatters

    def grad_normed_end(m, scatters):
        copies = []
        copies += grad_normed_sum(m, 0, scatters[0])
        copies += grad_normed_sum(m, 1, scatters[1])
        onward(scatters[2])
        copies += grad_normed_sum(m, 3, scatters[3])
        copies += grad_normed_sum(m, 2, scatters[2])
        grad_normed_back(m)
        for part in scatters.values():
            copies += part.copies
        return copies

    scatters = grad_normed(0)
    n_copies = grad_normed_end(0, scatters)
    grad_input(0)
    for i, j in blocks:
        send(
            pipe_src.at[i, :, cols_of(j)], up_own.at[1, j, :, cols_of(i)], pipe_sem.at[0], dev_p
        )
    att_gathers[1].forward()
    arrived(up_own.at[1], pipe_sem.at[0])

    spread_a(up_own, up_all, up_a_sem, 1)
    start_x(up_gathers[1], up_a_sem, up_all, 1)
    finish(g_copies)
    finish(n_copies)
    for step in (0, 2, 1, 3):
        up_gathers[1][step].forward()
    for gather in att_gathers + [nm_gathers[0][step] for step in range(RING)]:
        gather.near()
        gather.far()
    scatter = grad_attn_partial(1)
    start_x(nm_gathers[1], nm_a_sem, nm_all, 1)
    out_scatter = weight_rows(0, up_all, att_all, QCOLS, DCOLS)
    grad_attn_sum(1, scatter)
    backward(1)
    d_gathers[1].start()
    for step in range(RING):
        nm_gathers[1][step].forward()
    onward(out_scatter)
    scatters = grad_normed(1)
    for step in range(RING):
        nm_gathers[1][step].near()
        nm_gathers[1][step].far()
    qkv_scatter = weight_rows(1, nm_all, d_all, DCOLS, 0)
    grad_normed_end(1, scatters)
    onward(qkv_scatter)
    grad_input(1)

    gain_x[t] = gain_mine[...]
    for o in ORDER:
        send(gain_x.at[t], gain_x.at[t], gx_sem.at[t], dev_x(o))
    out_scatter.wait()
    for n in range(4):
        go_ref[:, cols_of(n)] = summed(pl.ds(DCOLS + n * BLOCK, BLOCK))
    for o in ORDER:
        arrived(gain_x.at[plus(t, o)], gx_sem.at[plus(t, o)])
    gain_a[a] = gain_x[0] + gain_x[1] + gain_x[2] + gain_x[3]
    for o in ORDER:
        send(gain_a.at[a], gain_a.at[a], ga_sem.at[a], dev_a(o))
    for o in ORDER:
        arrived(gain_a.at[plus(a, o)], ga_sem.at[plus(a, o)])
    gain_b[b] = gain_a[0] + gain_a[1] + gain_a[2] + gain_a[3]
    for o in ORDER:
        send(gain_b.at[b], gain_b.at[b], gb_sem.at[b], dev_b(o))
    for o in ORDER:
        arrived(gain_b.at[plus(b, o)], gb_sem.at[plus(b, o)])
    gain_mine[...] = gain_b[0] + gain_b[1] + gain_b[2] + gain_b[3]
    for i, j in blocks:
        gg_ref[:, at(dp_of(i, j), BLOCK)] = gain_mine[pl.ds(i * 2 + j // 2, 1), cols_of(j % 2)]

    qkv_scatter.wait()
    for n in range(4):
        gq_ref[:, cols_of(n)] = summed(cols_of(n))
    gk_ref[...] = summed(pl.ds(QCOLS, KVCOLS))
    gv_ref[...] = summed(pl.ds(QCOLS + KVCOLS, KVCOLS))
    finish(list(unfinished.values()))


def local(x_saved, grad_top, query, key, value, segment, w_query, key_weight, value_weight, w_out, gain):
    vmem = pl.BlockSpec(memory_space=pltpu.VMEM)
    hbm = pl.BlockSpec(memory_space=pl.ANY)
    dma = pltpu.SemaphoreType.DMA
    outs = pl.pallas_call(
        kernel,
        out_shape=(
            jax.ShapeDtypeStruct((SUB, WIDTH), BF16),
            jax.ShapeDtypeStruct((BLOCK, QCOLS), BF16),
            jax.ShapeDtypeStruct((BLOCK, KVCOLS), BF16),
            jax.ShapeDtypeStruct((BLOCK, KVCOLS), BF16),
            jax.ShapeDtypeStruct((BLOCK, QCOLS), BF16),
            jax.ShapeDtypeStruct((1, WIDTH), F32),
        ),
        in_specs=[hbm] * 5 + [vmem] * 2 + [hbm] * 4,
        out_specs=(vmem,) * 6,
        scratch_shapes=[
            pltpu.VMEM((2, SUB, WIDTH), BF16),
            pltpu.VMEM((2, TOK, QCOLS), BF16),
            pltpu.VMEM((2, TOK, KVCOLS), BF16),
            pltpu.VMEM((2, TOK, KVCOLS), BF16),
            pltpu.VMEM((2, RING, SUB, GROUP), BF16),
            pltpu.VMEM((2, RING, SUB, GROUP), BF16),
            pltpu.VMEM((2, GROUP, GROUP), BF16),
            pltpu.VMEM((2, GROUP, GROUP), BF16),
            pltpu.VMEM((GROUP, QCOLS), BF16),
            pltpu.VMEM((GROUP, DCOLS), BF16),
            pltpu.VMEM((2, GROUP, DCOLS), BF16),
            pltpu.VMEM((2, GROUP, QCOLS), BF16),
            pltpu.VMEM((RING, TOK, QCOLS), BF16),
            pltpu.VMEM((2, 2, TOK // 2, QCOLS), BF16),
            pltpu.VMEM((2, 2, TOK, QCOLS), BF16),
            pltpu.VMEM((TOK, QCOLS), BF16),
            pltpu.VMEM((2, 8, TOK, TOK), F32),
            pltpu.VMEM((RING, RING, SUB, GROUP), BF16),
            pltpu.VMEM((2, 2, RING, SUB // 2, GROUP), BF16),
            pltpu.VMEM((2, 2, RING, SUB, GROUP), BF16),
            pltpu.VMEM((RING, SUB, GROUP), BF16),
            pltpu.VMEM((2, RING, SUB, GROUP), BF16),
            pltpu.VMEM((RING, SUB, GROUP), BF16),
            pltpu.VMEM((RING, BLOCK, ALLCOLS), BF16),
            pltpu.VMEM((2, BLOCK // 2, ALLCOLS), BF16),
            pltpu.VMEM((2, BLOCK, ALLCOLS), BF16),
            pltpu.VMEM((2, SUB, HEAD), F32),
            pltpu.VMEM((8, 512), F32),
            pltpu.VMEM((RING, 8, 512), F32),
            pltpu.VMEM((RING, 8, 512), F32),
            pltpu.VMEM((RING, 8, 512), F32),
            dma((320,)),
            dma((2, RING)),
            dma((2, RING, RING, 2)),
            dma((2, RING)),
            dma((2, RING, RING, 2)),
            dma((2, RING, 2)),
            dma((2, 2)),
            dma((2, 2, 2)),
            dma((2, RING, 2)),
            dma((2, RING, 2)),
            dma((2, 2, RING)),
            dma((2, 2, RING, 2)),
            dma((2, RING)),
            dma((1,)),
            dma((2, 2)),
            dma((2, 2, 2)),
            dma((RING,)),
            dma((RING,)),
            dma((RING,)),
            dma((9,)),
        ],
        compiler_params=pltpu.CompilerParams(
            collective_id=0, has_side_effects=True, vmem_limit_bytes=63 * 2**20
        ),
        cost_estimate=pl.CostEstimate(flops=23 * 10**9, bytes_accessed=8 * 10**6, transcendentals=10**6),
        name="relay_backward",
    )(
        x_saved[0, 0], grad_top[0, 0], query[0, 0], key[0, 0], value[0, 0], segment[0, 0], gain,
        w_query[0], key_weight[0], value_weight[0], w_out[0],
    )
    bottom, gq, gk, gv, go, gg = outs
    return (bottom[None, None], gq[None], gk[None], gv[None], go[None], gg)


def solution(mesh):
    in_specs = (
        P("pipe", "dp", None, "tensor", None),
        P("pipe", "dp", "tensor", None),
        P("pipe", "dp", None, None, "tensor"),
        P("pipe", "dp", None, None, "tensor"),
        P("pipe", "dp", None, None, "tensor"),
        P("pipe", "dp", None, None),
        P("pipe", "dp", "tensor"),
        P("pipe", "dp", "tensor"),
        P("pipe", "dp", "tensor"),
        P("pipe", "dp", "tensor"),
        P("pipe", None),
    )
    out_specs = (
        P("pipe", "dp", "tensor", None),
        P("pipe", "dp", "tensor"),
        P("pipe", "dp", "tensor"),
        P("pipe", "dp", "tensor"),
        P("pipe", "dp", "tensor"),
        P("pipe", None),
    )
    return jax.shard_map(local, mesh=mesh, in_specs=in_specs, out_specs=out_specs, check_vma=False)
```

```python
import functools
import math

import jax
import jax.numpy as jnp
from jax import lax
from jax.experimental import pallas as pl
from jax.experimental.pallas import tpu as pltpu
from jax.sharding import PartitionSpec as P

BF16 = jnp.bfloat16
F32 = jnp.float32
MESH = pl.DeviceIdType.MESH
HEAD = 128
EPS = 1e-05
RING = 4
TOK = 256
SUB = 64
WIDTH = 4096
GROUP = 1024
BLOCK = 256
QCOLS = 1024
KVCOLS = 256
DCOLS = QCOLS + 2 * KVCOLS
ALLCOLS = DCOLS + QCOLS
SCALE = 1.0 / math.sqrt(HEAD)
ORDER = (1, 3, 2)
PART = 32


def nn(left, right):
    return lax.dot_general(left, right, (((1,), (0,)), ((), ())), preferred_element_type=F32)


def nt(left, right):
    return lax.dot_general(left, right, (((1,), (1,)), ((), ())), preferred_element_type=F32)


def tn(left, right):
    return lax.dot_general(left, right, (((0,), (0,)), ((), ())), preferred_element_type=F32)


def at(index, size):
    return pl.ds(pl.multiple_of(index * size, size), size)


def kernel(
    x_hbm, top_hbm, q_hbm, k_hbm, v_hbm, seg_ref, gain_ref, wq_ref, wk_ref, wv_ref, wo_ref,
    bottom_ref, gq_ref, gk_ref, gv_ref, go_ref, gg_ref,
    x_ref, q_ref, k_ref, v_ref,
    up_own, nm_own, up_all, nm_all, w_out, w_qkv, d_all, att_all,
    g_part, g_relay, g_recv, g_own, probs,
    n_part, n_relay, n_recv, n_far, n_sum, f_recv, pipe_src, p_early, p_part, p_relay, p_recv, inv_ref,
    gain_mine, gain_x, gain_a, gain_b,
    send_sem, up_a_sem, up_x_sem, nm_a_sem, nm_x_sem, w_sem, gr_sem, g_sem, d_sem, att_sem,
    nr_sem, n_sem, nf_sem, f_sem, pipe_sem, pr_sem, p_sem, gx_sem, ga_sem, gb_sem, local_sem,
):
    p = lax.axis_index("pipe")
    t = lax.axis_index("tensor")
    dp = lax.axis_index("dp")
    z = lax.div(dp, RING)
    y = lax.rem(dp, RING)
    a = (1 - p) * z + p * y
    b = (1 - p) * y + p * z

    def dp_of(aa, bb):
        return (1 - p) * (RING * aa + bb) + p * (RING * bb + aa)

    def plus(i, o):
        return lax.rem(i + o, RING)

    def dev_x(o):
        return (p, plus(t, o), dp)

    def dev_a(o):
        return (p, t, dp_of(plus(a, o), b))

    def dev_b(o):
        return (p, t, dp_of(a, plus(b, o)))

    dev_p = (1 - p, t, dp)

    sends = []
    unfinished = {}

    def send(src, dst, recv_sem, device):
        copy = pltpu.make_async_remote_copy(
            src_ref=src, dst_ref=dst, send_sem=send_sem.at[len(sends)], recv_sem=recv_sem,
            device_id=device, device_id_type=MESH,
        )
        copy.start()
        sends.append(copy)
        unfinished[id(copy)] = copy
        return copy

    def finish(copies):
        for copy in copies:
            copy.wait_send()
            del unfinished[id(copy)]

    def arrived(dst, recv_sem):
        pltpu.make_async_remote_copy(
            src_ref=dst, dst_ref=dst, send_sem=send_sem.at[0], recv_sem=recv_sem,
            device_id=dev_p, device_id_type=MESH,
        ).wait_recv()

    class Gather:
        def __init__(self, view, sem, me, device):
            self.view, self.sem, self.me, self.device = view, sem, me, device

        def copy(self, owner, half, way):
            place = self.view(owner, half)
            send(place, place, self.sem(owner, half), self.device(way))

        def wait(self, owner, half):
            arrived(self.view(owner, half), self.sem(owner, half))

        def start(self):
            for half, way in ((0, 1), (1, 3), (1, 1), (0, 3)):
                self.copy(self.me, half, way)

        def forward(self):
            for half, origin, way in ((0, 3, 1), (1, 1, 3)):
                owner = plus(self.me, origin)
                self.wait(owner, half)
                self.copy(owner, half, way)

        def near(self):
            self.wait(plus(self.me, 3), 1)
            self.wait(plus(self.me, 1), 0)

        def far(self):
            self.wait(plus(self.me, 2), 0)
            self.wait(plus(self.me, 2), 1)

    class Scatter:
        def __init__(self, part, relay, recv, relay_sem, sem, me, device):
            self.part, self.relay, self.recv = part, relay, recv
            self.relay_sem, self.sem, self.me, self.device = relay_sem, sem, me, device
            self.copies = []

        def far(self):
            for half, way in ((0, 1), (1, 3)):
                self.copies.append(
                    send(self.part(plus(self.me, 2), half), self.relay(half), self.relay_sem(half),
                         self.device(way))
                )

        def direct(self, half):
            way, other = ((1, 3)[half], 1 - half)
            self.copies.append(
                send(self.part(plus(self.me, way), other), self.recv(half, other),
                     self.sem(half, other), self.device(way))
            )

        def onward(self, half):
            way = (1, 3)[half]
            arrived(self.relay(half), self.relay_sem(half))
            place = self.part(plus(self.me, way), half)
            place[...] = (place[...].astype(F32) + self.relay(half)[...].astype(F32)).astype(BF16)
            self.copies.append(
                send(place, self.recv(half, half), self.sem(half, half), self.device(way))
            )

        def wait(self):
            for way in range(2):
                for half in range(2):
                    arrived(self.recv(way, half), self.sem(way, half))

    barrier = pltpu.get_barrier_semaphore()
    partners = [f(o) for f in (dev_x, dev_a, dev_b) for o in ORDER] + [dev_p]
    partners += [(1 - p, t, dp_of(plus(a, o), b)) for o in ORDER]
    for device in partners:
        pl.semaphore_signal(barrier, inc=1, device_id=device, device_id_type=MESH)

    blocks = [(i, j) for i in range(RING) for j in range(RING)]

    def cols_of(j):
        return pl.ds(j * BLOCK, BLOCK)

    for i, j in blocks:
        pltpu.make_async_copy(
            top_hbm.at[:, at(dp_of(i, j), BLOCK)], up_own.at[0, i, :, cols_of(j)], local_sem.at[0]
        ).start()
    loads = [
        pltpu.make_async_copy(x_hbm, x_ref, local_sem.at[1]),
        pltpu.make_async_copy(q_hbm, q_ref, local_sem.at[2]),
        pltpu.make_async_copy(k_hbm, k_ref, local_sem.at[3]),
        pltpu.make_async_copy(v_hbm, v_ref, local_sem.at[4]),
        pltpu.make_async_copy(wo_ref, w_out.at[at(b, BLOCK), :], local_sem.at[5]),
        pltpu.make_async_copy(wq_ref, w_qkv.at[at(b, BLOCK), pl.ds(0, QCOLS)], local_sem.at[6]),
        pltpu.make_async_copy(
            wk_ref, w_qkv.at[at(b, BLOCK), pl.ds(QCOLS, KVCOLS)], local_sem.at[7]
        ),
        pltpu.make_async_copy(
            wv_ref, w_qkv.at[at(b, BLOCK), pl.ds(QCOLS + KVCOLS, KVCOLS)], local_sem.at[8]
        ),
    ]
    for copy in loads:
        copy.start()
    pltpu.make_async_copy(up_own.at[0], up_own.at[0], local_sem.at[0]).wait()
    pl.semaphore_wait(barrier, len(partners))

    rows_own = at(a, TOK)

    def half_rows(i, half, size):
        return pl.ds(pl.multiple_of(i * size + half * (size // 2), size // 2), size // 2)

    def slab(i):
        return pl.ds(pl.multiple_of(i * TOK + t * SUB, SUB), SUB)

    def part_rows(i, owner, h):
        return pl.ds(pl.multiple_of(i * TOK + owner * SUB + h * PART, PART), PART)

    def own_part(h):
        return pl.ds(h * PART, PART)

    def spread_nm(m):
        for o in ORDER:
            send(nm_own.at[m, plus(a, o)], nm_all.at[m, slab(a), :], nm_a_sem.at[m, a], dev_a(o))
        nm_all[m, slab(a), :] = nm_own[m, a]

    def spread_up(h):
        for o in ORDER:
            send(
                up_own.at[0, plus(a, o), own_part(h), :], up_all.at[0, part_rows(a, t, h), :],
                up_a_sem.at[0, a, h], dev_a(o),
            )
        up_all[0, part_rows(a, t, h), :] = up_own[0, a, own_part(h), :]

    def up_gather(m, step, h):
        i = plus(a, step)

        def view(owner, half):
            start = i * TOK + owner * SUB + h * PART + half * (PART // 2)
            return up_all.at[m, pl.ds(pl.multiple_of(start, PART // 2), PART // 2), :]

        return Gather(view, lambda owner, half: up_x_sem.at[m, i, h, owner, half], t, dev_x)

    def nm_gather(m, step):
        i = plus(a, step)

        def view(owner, half):
            start = i * TOK + owner * SUB + half * (SUB // 2)
            return nm_all.at[m, pl.ds(pl.multiple_of(start, SUB // 2), SUB // 2), :]

        return Gather(view, lambda owner, half: nm_x_sem.at[m, i, owner, half], t, dev_x)

    def d_gather(m, h):
        return Gather(
            lambda owner, half: d_all.at[m, owner, pl.ds(2 * half, 2), h],
            lambda owner, half: d_sem.at[m, h, owner, half], a, dev_a,
        )

    def row_gather(ref, sem, m):
        return Gather(
            lambda owner, half: ref.at[m, half_rows(owner, half, TOK), :],
            lambda owner, half: sem.at[m, owner, half], a, dev_a,
        )

    def weight_gather(ref, cols, index):
        return Gather(
            lambda owner, half: ref.at[half_rows(owner, half, BLOCK), cols],
            lambda owner, half: w_sem.at[index, owner, half], b, dev_b,
        )

    out_gather = weight_gather(w_out, slice(None), 0)
    qkv_gather = weight_gather(w_qkv, slice(None), 1)
    up_gathers = [
        {(step, h): up_gather(m, step, h) for step in range(RING) for h in range(2)}
        for m in range(2)
    ]
    nm_gathers = [[nm_gather(m, step) for step in range(RING)] for m in range(2)]
    d_gathers = [[d_gather(m, h) for h in range(2)] for m in range(2)]
    att_gathers = [row_gather(att_all, att_sem, m) for m in range(2)]

    def nm_start(m, step):
        i = plus(a, step)
        if step:
            arrived(nm_all.at[m, slab(i), :], nm_a_sem.at[m, i])
        nm_gathers[m][step].start()

    def norm(m):
        square = jnp.zeros((SUB, 1), F32)
        for f in range(16):
            x = x_ref[m, :, cols_of(f)].astype(F32)
            square = square + jnp.sum(x * x, axis=-1, keepdims=True)
        inv = lax.rsqrt(square * (1.0 / WIDTH) + EPS)
        inv_ref[m] = jnp.broadcast_to(inv, (SUB, HEAD))
        for i, j in blocks:
            feature = at(dp_of(i, j), BLOCK)
            x = x_ref[m, :, feature].astype(F32)
            nm_own[m, i, :, cols_of(j)] = (x * inv * gain_ref[:, feature]).astype(BF16)

    def forward(m):
        seg_row = jnp.broadcast_to(seg_ref[m : m + 1, :], (TOK, TOK)).astype(F32)
        seg_col = jnp.transpose(seg_row)
        row = lax.broadcasted_iota(jnp.int32, (TOK, TOK), 0)
        col = lax.broadcasted_iota(jnp.int32, (TOK, TOK), 1)
        allowed = (row <= col) & (seg_row == seg_col)
        bias = jnp.where(allowed, 0.0, -1e30).astype(F32)

        def group(g, carry):
            key = k_ref[m, :, at(g, HEAD)]
            value = v_ref[m, :, at(g, HEAD)]
            for h in range(RING):
                cols = at(g * RING + h, HEAD)
                scores = nt(key, q_ref[m, :, cols]) * SCALE + bias
                top = jnp.max(scores, axis=0, keepdims=True)
                raised = jnp.exp(scores - top)
                attention = raised * (1.0 / jnp.sum(raised, axis=0, keepdims=True))
                probs[m, g * RING + h] = attention
                att_all[m, rows_own, cols] = tn(attention.astype(BF16), value).astype(BF16)
            return carry

        lax.fori_loop(0, 2, group, 0)

    def grad_attn_rows(m, i, dst):
        def chunk(n, carry):
            cols = at(n, BLOCK)
            dst[:, cols] = nn(up_all[m, at(i, TOK), :], w_out[:, cols]).astype(BF16)
            return carry

        lax.fori_loop(0, RING, chunk, 0)

    def grad_attn_scatter(m):
        return Scatter(
            lambda dest, half: g_part.at[dest, pl.ds(half * 128, 128), :],
            lambda way: g_relay.at[way],
            lambda way, half: g_recv.at[way, pl.ds(half * 128, 128), :],
            lambda way: gr_sem.at[m, way],
            lambda way, half: g_sem.at[m, way, half],
            a, dev_a,
        )

    UNITS = ((0, 0), (1, 0), (3, 0), (2, 0), (2, 1), (1, 1), (3, 1), (0, 1))

    def up_start(m, units):
        for step, h in units:
            i = plus(a, step)
            if m or step:
                arrived(up_all.at[m, part_rows(i, t, h), :], up_a_sem.at[m, i, h])
            up_gathers[m][step, h].start()

    def up_forward(m, units):
        for unit in units:
            up_gathers[m][unit].forward()

    def grad_attn_partial(m):
        scatter = grad_attn_scatter(m)

        def rows(step):
            for h in range(2):
                up_gathers[m][step, h].near()
                up_gathers[m][step, h].far()
            i = plus(a, step)
            grad_attn_rows(m, i, g_part.at[i])

        rows(2)
        scatter.far()
        rows(1)
        scatter.direct(0)
        rows(3)
        scatter.direct(1)
        rows(0)
        return scatter

    def grad_attn_sum(m, scatter):
        scatter.wait()
        for n in range(RING):
            cols = cols_of(n)
            total = g_part[a, :, cols].astype(F32) + g_recv[0, :, cols].astype(F32)
            g_own[:, cols] = (total + g_recv[1, :, cols].astype(F32)).astype(BF16)

    def backward(m):
        def put(cols, value):
            d_all[m, a, :, :, :, cols] = value.astype(BF16).reshape(RING, 2, PART, HEAD)

        def group(g, carry):
            key = k_ref[m, :, at(g, HEAD)]
            value = v_ref[m, :, at(g, HEAD)]
            dk = jnp.zeros((TOK, HEAD), F32)
            dv = jnp.zeros((TOK, HEAD), F32)
            for h in range(RING):
                cols = at(g * RING + h, HEAD)
                grad = g_own[:, cols]
                attention = probs[m, g * RING + h]
                grad_probs = nt(value, grad)
                row_dot = jnp.sum(attention * grad_probs, axis=0, keepdims=True)
                score = (attention * (grad_probs - row_dot) * SCALE).astype(BF16)
                put(cols, tn(score, key))
                dk = dk + nn(score, q_ref[m, :, cols])
                dv = dv + nn(attention.astype(BF16), grad)
            put(pl.ds(pl.multiple_of(QCOLS + g * HEAD, HEAD), HEAD), dk)
            put(pl.ds(pl.multiple_of(QCOLS + KVCOLS + g * HEAD, HEAD), HEAD), dv)
            return carry

        lax.fori_loop(0, 2, group, 0)

    def grad_normed_rows(m, step, h):
        i = plus(a, step)

        def chunk(n, carry):
            cols = at(n, BLOCK)
            left = d_all[m, i, :, h].reshape(RING * PART, DCOLS)
            part = nt(left, w_qkv[at(n, BLOCK), :]).astype(BF16)
            for u in range(RING):
                n_part[u, i, h, :, cols] = part[u * PART : (u + 1) * PART, :]
            return carry

        lax.fori_loop(0, RING, chunk, 0)
        if step == 2:
            copies = [
                send(n_part.at[plus(t, 2), i, h], n_far.at[m, h], nf_sem.at[m, h], dev_x(2)),
                send(n_part.at[plus(t, 1), i, h], n_recv.at[m, 0, i, h], n_sem.at[m, 0, i, h, 0], dev_x(1)),
                send(n_part.at[plus(t, 3), i, h], n_recv.at[m, 1, i, h], n_sem.at[m, 1, i, h, 0], dev_x(3)),
            ]
            n_copies.extend(copies)
            return None
        scatter = Scatter(
            lambda dest, half: n_part.at[dest, i, h, pl.ds(half * 16, 16), :],
            lambda way: n_relay.at[m, way, i, h],
            lambda way, half: n_recv.at[m, way, i, h, pl.ds(half * 16, 16), :],
            lambda way: nr_sem.at[m, way, i, h],
            lambda way, half: n_sem.at[m, way, i, h, half],
            t, dev_x,
        )
        scatter.copies = n_copies
        scatter.far()
        scatter.direct(0)
        scatter.direct(1)
        return scatter

    def onward(scatter):
        scatter.onward(0)
        scatter.onward(1)

    def grad_normed_sum(m, step, h, scatter):
        i = plus(a, step)
        if step == 2:
            arrived(n_recv.at[m, 0, i, h], n_sem.at[m, 0, i, h, 0])
            arrived(n_recv.at[m, 1, i, h], n_sem.at[m, 1, i, h, 0])
            arrived(n_far.at[m, h], nf_sem.at[m, h])
        else:
            scatter.wait()
        for n in range(RING):
            cols = cols_of(n)
            total = n_part[t, i, h, :, cols].astype(F32) + n_recv[m, 0, i, h, :, cols].astype(F32)
            total = total + n_recv[m, 1, i, h, :, cols].astype(F32)
            if step == 2:
                total = total + n_far[m, h, :, cols].astype(F32)
            if step:
                n_sum[i, h, :, cols] = total.astype(BF16)
            else:
                f_recv[m, i, h, :, cols] = total.astype(BF16)
        if step:
            n_copies.append(
                send(n_sum.at[i, h], f_recv.at[m, a, h], f_sem.at[m, a, h], dev_a(step))
            )

    def grad_normed_back(m, h):
        for o in ORDER:
            arrived(f_recv.at[m, plus(a, o), h], f_sem.at[m, plus(a, o), h])

    def grad_input(m, h):
        rows = own_part(h)
        inv = inv_ref[m, rows, :][:, :1]
        total = jnp.zeros((PART, 1), F32)
        for i, j in blocks:
            feature = at(dp_of(i, j), BLOCK)
            unit = x_ref[m, rows, feature].astype(F32) * inv
            grad = f_recv[m, i, h, :, cols_of(j)].astype(F32)
            term = unit * grad
            total = total + jnp.sum(term * gain_ref[:, feature], axis=-1, keepdims=True)
            place = (pl.ds(i * 2 + j // 2, 1), cols_of(j % 2))
            gain_sum = jnp.sum(term, axis=0, keepdims=True)
            if m == 0 and h == 0:
                gain_mine[place] = gain_sum
            else:
                gain_mine[place] = gain_mine[place] + gain_sum
        mean = total * (1.0 / WIDTH)
        for i, j in blocks:
            feature = at(dp_of(i, j), BLOCK)
            unit = x_ref[m, rows, feature].astype(F32) * inv
            grad = f_recv[m, i, h, :, cols_of(j)].astype(F32)
            result = up_own[m, i, rows, cols_of(j)].astype(F32) + inv * (
                gain_ref[:, feature] * grad - unit * mean
            )
            if m == 0:
                pipe_src[j, rows, cols_of(i)] = result.astype(BF16)
            else:
                bottom_ref[rows, feature] = result.astype(BF16)

    def hand_down(h):
        rows = own_part(h)
        for o in (0,) + ORDER:
            j = plus(b, o)
            send(
                pipe_src.at[j, rows, :], up_all.at[1, part_rows(b, t, h), :],
                up_a_sem.at[1, b, h], (1 - p, t, dp_of(a, j)),
            )
        send(pipe_src.at[:, rows, :], up_own.at[1, :, rows, :], pipe_sem.at[h], dev_p)

    def weight_scatter(first, offset, width):
        return Scatter(
            lambda dest, half: p_part.at[dest, pl.ds(half * 128, 128), pl.ds(offset, width)],
            lambda way: p_relay.at[way, :, pl.ds(offset, width)],
            lambda way, half: p_recv.at[way, pl.ds(half * 128, 128), pl.ds(offset, width)],
            lambda way: pr_sem.at[first, way],
            lambda way, half: p_sem.at[first, way, half],
            b, dev_b,
        )

    def out_rows(step):
        j = plus(b, step)
        feature = at(j, BLOCK)

        def chunk(n, carry):
            cols = at(n, 512)
            total = tn(up_all[0, :, feature], att_all[0, :, cols])
            total = total + tn(up_all[1, :, feature], att_all[1, :, cols])
            place = pl.ds(pl.multiple_of(DCOLS + n * 512, 512), 512)
            p_part[j, :, place] = total.astype(BF16)
            return carry

        lax.fori_loop(0, QCOLS // 512, chunk, 0)

    def qkv_rows(m, step):
        j = plus(b, step)
        feature = at(j, BLOCK)

        def chunk(n, carry):
            cols = at(n, 512)
            total = tn(nm_all[m, :, feature], d_all[m, :, :, :, :, cols].reshape(GROUP, 512))
            if m == 0:
                p_early[j, :, cols] = total
            else:
                p_part[j, :, cols] = (p_early[j, :, cols] + total).astype(BF16)
            return carry

        lax.fori_loop(0, DCOLS // 512, chunk, 0)

    def summed(cols):
        total = p_part[b, :, cols].astype(F32) + p_recv[0, :, cols].astype(F32)
        return (total + p_recv[1, :, cols].astype(F32)).astype(BF16)

    n_copies = []
    out_scatter = weight_scatter(0, DCOLS, QCOLS)
    qkv_scatter = weight_scatter(1, 0, DCOLS)

    spread_up(0)
    spread_up(1)
    up_start(0, UNITS[:1])
    loads[4].wait()
    out_gather.start()
    loads[0].wait()
    norm(0)
    up_start(0, UNITS[1:])
    for copy in loads[1:4]:
        copy.wait()
    forward(0)
    att_gathers[0].start()
    spread_nm(0)
    for copy in loads[5:]:
        copy.wait()
    out_gather.forward()
    qkv_gather.start()
    up_forward(0, UNITS[:4])
    norm(1)
    spread_nm(1)
    forward(1)
    up_forward(0, UNITS[4:])
    att_gathers[0].forward()
    out_gather.near()
    out_gather.far()
    scatter = grad_attn_partial(0)
    g_copies = scatter.copies
    for step in (0, 1, 3, 2):
        nm_start(0, step)
    onward(scatter)
    qkv_gather.forward()
    grad_attn_sum(0, scatter)
    backward(0)

    def grad_normed(m):
        first, second = d_gathers[m]
        first.start()
        second.start()
        if m == 0:
            qkv_gather.near()
            qkv_gather.far()
        parts = {(0, 0): grad_normed_rows(m, 0, 0), (0, 1): grad_normed_rows(m, 0, 1)}
        first.forward()
        for step in (0, 1, 3, 2):
            nm_gathers[m][step].forward()
        first.near()
        parts[1, 0] = grad_normed_rows(m, 1, 0)
        parts[3, 0] = grad_normed_rows(m, 3, 0)
        onward(parts[0, 0])
        onward(parts[0, 1])
        second.forward()
        first.far()
        parts[2, 0] = grad_normed_rows(m, 2, 0)
        onward(parts[1, 0])
        onward(parts[3, 0])
        second.near()
        parts[1, 1] = grad_normed_rows(m, 1, 1)
        parts[3, 1] = grad_normed_rows(m, 3, 1)
        for step in (0, 1, 3, 2):
            grad_normed_sum(m, step, 0, parts[step, 0])
        second.far()
        parts[2, 1] = grad_normed_rows(m, 2, 1)
        onward(parts[1, 1])
        onward(parts[3, 1])
        return parts

    parts = grad_normed(0)
    grad_normed_back(0, 0)
    grad_input(0, 0)
    hand_down(0)
    for step in (0, 1, 3, 2):
        grad_normed_sum(0, step, 1, parts[step, 1])
    up_start(1, UNITS[:4])
    for gather in nm_gathers[0]:
        gather.near()
        gather.far()
    qkv_rows(0, 2)
    qkv_rows(0, 1)
    grad_normed_back(0, 1)
    grad_input(0, 1)
    hand_down(1)
    up_forward(1, UNITS[:4])
    att_gathers[1].start()
    qkv_rows(0, 3)
    qkv_rows(0, 0)

    up_start(1, UNITS[4:])
    up_forward(1, UNITS[4:])
    att_gathers[1].forward()
    finish(g_copies)
    scatter = grad_attn_partial(1)
    for step in (0, 1, 3, 2):
        nm_start(1, step)
    onward(scatter)
    for gather in att_gathers:
        gather.near()
        gather.far()
    out_rows(2)
    out_scatter.far()
    out_rows(1)
    out_scatter.direct(0)
    out_rows(3)
    out_scatter.direct(1)
    grad_attn_sum(1, scatter)
    backward(1)
    finish(n_copies)
    parts = grad_normed(1)
    onward(out_scatter)
    for gather in nm_gathers[1]:
        gather.near()
        gather.far()
    qkv_rows(1, 2)
    qkv_scatter.far()
    qkv_rows(1, 1)
    qkv_scatter.direct(0)
    qkv_rows(1, 3)
    qkv_scatter.direct(1)
    for h in range(2):
        arrived(up_own.at[1, :, own_part(h), :], pipe_sem.at[h])
    grad_normed_back(1, 0)
    grad_input(1, 0)
    for step in (0, 1, 3, 2):
        grad_normed_sum(1, step, 1, parts[step, 1])
    onward(qkv_scatter)
    out_rows(0)
    qkv_rows(1, 0)
    grad_normed_back(1, 1)
    grad_input(1, 1)

    gain_x[t] = gain_mine[...]
    for o in ORDER:
        send(gain_x.at[t], gain_x.at[t], gx_sem.at[t], dev_x(o))
    out_scatter.wait()
    for n in range(4):
        go_ref[:, cols_of(n)] = summed(pl.ds(DCOLS + n * BLOCK, BLOCK))
    for o in ORDER:
        arrived(gain_x.at[plus(t, o)], gx_sem.at[plus(t, o)])
    gain_a[a] = gain_x[0] + gain_x[1] + gain_x[2] + gain_x[3]
    for o in ORDER:
        send(gain_a.at[a], gain_a.at[a], ga_sem.at[a], dev_a(o))
    for o in ORDER:
        arrived(gain_a.at[plus(a, o)], ga_sem.at[plus(a, o)])
    gain_b[b] = gain_a[0] + gain_a[1] + gain_a[2] + gain_a[3]
    for o in ORDER:
        send(gain_b.at[b], gain_b.at[b], gb_sem.at[b], dev_b(o))
    for o in ORDER:
        arrived(gain_b.at[plus(b, o)], gb_sem.at[plus(b, o)])
    gain_mine[...] = gain_b[0] + gain_b[1] + gain_b[2] + gain_b[3]
    for i, j in blocks:
        gg_ref[:, at(dp_of(i, j), BLOCK)] = gain_mine[pl.ds(i * 2 + j // 2, 1), cols_of(j % 2)]

    qkv_scatter.wait()
    for n in range(4):
        gq_ref[:, cols_of(n)] = summed(cols_of(n))
    gk_ref[...] = summed(pl.ds(QCOLS, KVCOLS))
    gv_ref[...] = summed(pl.ds(QCOLS + KVCOLS, KVCOLS))
    finish(list(unfinished.values()))


def hand_out(*refs):
    for src, dst in zip(refs[:6], refs[6:]):
        dst[...] = src[...]


def local(x_saved, grad_top, query, key, value, segment, w_query, key_weight, value_weight, w_out, gain):
    vmem = pl.BlockSpec(memory_space=pltpu.VMEM)
    hbm = pl.BlockSpec(memory_space=pl.ANY)
    dma = pltpu.SemaphoreType.DMA
    outs = pl.pallas_call(
        kernel,
        out_shape=(
            jax.ShapeDtypeStruct((SUB, WIDTH), BF16),
            jax.ShapeDtypeStruct((BLOCK, QCOLS), BF16),
            jax.ShapeDtypeStruct((BLOCK, KVCOLS), BF16),
            jax.ShapeDtypeStruct((BLOCK, KVCOLS), BF16),
            jax.ShapeDtypeStruct((BLOCK, QCOLS), BF16),
            jax.ShapeDtypeStruct((1, WIDTH), F32),
        ),
        in_specs=[hbm] * 5 + [vmem] * 2 + [hbm] * 4,
        out_specs=(vmem,) * 6,
        scratch_shapes=[
            pltpu.VMEM((2, SUB, WIDTH), BF16),
            pltpu.VMEM((2, TOK, QCOLS), BF16),
            pltpu.VMEM((2, TOK, KVCOLS), BF16),
            pltpu.VMEM((2, TOK, KVCOLS), BF16),
            pltpu.VMEM((2, RING, SUB, GROUP), BF16),
            pltpu.VMEM((2, RING, SUB, GROUP), BF16),
            pltpu.VMEM((2, GROUP, GROUP), BF16),
            pltpu.VMEM((2, GROUP, GROUP), BF16),
            pltpu.VMEM((GROUP, QCOLS), BF16),
            pltpu.VMEM((GROUP, DCOLS), BF16),
            pltpu.VMEM((2, RING, RING, 2, PART, DCOLS), BF16),
            pltpu.VMEM((2, GROUP, QCOLS), BF16),
            pltpu.VMEM((RING, TOK, QCOLS), BF16),
            pltpu.VMEM((2, TOK // 2, QCOLS), BF16),
            pltpu.VMEM((2, TOK, QCOLS), BF16),
            pltpu.VMEM((TOK, QCOLS), BF16),
            pltpu.VMEM((2, 8, TOK, TOK), F32),
            pltpu.VMEM((RING, RING, 2, PART, GROUP), BF16),
            pltpu.VMEM((2, 2, RING, 2, PART // 2, GROUP), BF16),
            pltpu.VMEM((2, 2, RING, 2, PART, GROUP), BF16),
            pltpu.VMEM((2, 2, PART, GROUP), BF16),
            pltpu.VMEM((RING, 2, PART, GROUP), BF16),
            pltpu.VMEM((2, RING, 2, PART, GROUP), BF16),
            pltpu.VMEM((RING, SUB, GROUP), BF16),
            pltpu.VMEM((RING, BLOCK, DCOLS), F32),
            pltpu.VMEM((RING, BLOCK, ALLCOLS), BF16),
            pltpu.VMEM((2, BLOCK // 2, ALLCOLS), BF16),
            pltpu.VMEM((2, BLOCK, ALLCOLS), BF16),
            pltpu.VMEM((2, SUB, HEAD), F32),
            pltpu.VMEM((8, 512), F32),
            pltpu.VMEM((RING, 8, 512), F32),
            pltpu.VMEM((RING, 8, 512), F32),
            pltpu.VMEM((RING, 8, 512), F32),
            dma((400,)),
            dma((2, RING, 2)),
            dma((2, RING, 2, RING, 2)),
            dma((2, RING)),
            dma((2, RING, RING, 2)),
            dma((2, RING, 2)),
            dma((2, 2)),
            dma((2, 2, 2)),
            dma((2, 2, RING, 2)),
            dma((2, RING, 2)),
            dma((2, 2, RING, 2)),
            dma((2, 2, RING, 2, 2)),
            dma((2, 2)),
            dma((2, RING, 2)),
            dma((2,)),
            dma((2, 2)),
            dma((2, 2, 2)),
            dma((RING,)),
            dma((RING,)),
            dma((RING,)),
            dma((9,)),
        ],
        compiler_params=pltpu.CompilerParams(
            collective_id=0, has_side_effects=True, vmem_limit_bytes=63 * 2**20
        ),
        cost_estimate=pl.CostEstimate(flops=23 * 10**9, bytes_accessed=8 * 10**6, transcendentals=10**6),
        name="relay_backward",
    )(
        x_saved[0, 0], grad_top[0, 0], query[0, 0], key[0, 0], value[0, 0], segment[0, 0], gain,
        w_query[0], key_weight[0], value_weight[0], w_out[0],
    )
    bottom, gq, gk, gv, go, gg = pl.pallas_call(
        hand_out,
        out_shape=tuple(jax.ShapeDtypeStruct(out.shape, out.dtype) for out in outs),
        in_specs=[vmem] * 6,
        out_specs=(vmem,) * 6,
        name="hand_out",
    )(*outs)
    return (bottom[None, None], gq[None], gk[None], gv[None], go[None], gg)


def solution(mesh):
    in_specs = (
        P("pipe", "dp", None, "tensor", None),
        P("pipe", "dp", "tensor", None),
        P("pipe", "dp", None, None, "tensor"),
        P("pipe", "dp", None, None, "tensor"),
        P("pipe", "dp", None, None, "tensor"),
        P("pipe", "dp", None, None),
        P("pipe", "dp", "tensor"),
        P("pipe", "dp", "tensor"),
        P("pipe", "dp", "tensor"),
        P("pipe", "dp", "tensor"),
        P("pipe", None),
    )
    out_specs = (
        P("pipe", "dp", "tensor", None),
        P("pipe", "dp", "tensor"),
        P("pipe", "dp", "tensor"),
        P("pipe", "dp", "tensor"),
        P("pipe", "dp", "tensor"),
        P("pipe", None),
    )
    return jax.shard_map(local, mesh=mesh, in_specs=in_specs, out_specs=out_specs, check_vma=False)
```

```python
import functools
import math

import jax
import jax.numpy as jnp
from jax import lax
from jax.experimental import pallas as pl
from jax.experimental.pallas import tpu as pltpu
from jax.sharding import PartitionSpec as P

BF16 = jnp.bfloat16
F32 = jnp.float32
MESH = pl.DeviceIdType.MESH
HEAD = 128
EPS = 1e-05
RING = 4
TOK = 256
SUB = 64
WIDTH = 4096
GROUP = 1024
BLOCK = 256
QCOLS = 1024
KVCOLS = 256
DCOLS = QCOLS + 2 * KVCOLS
ALLCOLS = DCOLS + QCOLS
SCALE = 1.0 / math.sqrt(HEAD)
ORDER = (1, 3, 2)
PART = 32


def nn(left, right):
    return lax.dot_general(left, right, (((1,), (0,)), ((), ())), preferred_element_type=F32)


def nt(left, right):
    return lax.dot_general(left, right, (((1,), (1,)), ((), ())), preferred_element_type=F32)


def tn(left, right):
    return lax.dot_general(left, right, (((0,), (0,)), ((), ())), preferred_element_type=F32)


def at(index, size):
    return pl.ds(pl.multiple_of(index * size, size), size)


def kernel(
    x_hbm, top_hbm, q_hbm, k_hbm, v_hbm, seg_ref, gain_ref, wq_ref, wk_ref, wv_ref, wo_ref,
    bottom_ref, gq_ref, gk_ref, gv_ref, go_ref, gg_ref,
    x_ref, q_ref, k_ref, v_ref,
    up_own, nm_own, up_all, nm_all, w_out, w_qkv, d_all, att_all,
    g_part, g_relay, g_recv, g_own, probs,
    n_part, n_relay, n_recv, n_far, n_sum, f_recv, pipe_src, p_early, p_part, p_relay, p_recv, inv_ref,
    gain_mine, gain_x, gain_a, gain_b,
    send_sem, up_a_sem, up_x_sem, nm_a_sem, nm_x_sem, w_sem, gr_sem, g_sem, d_sem, att_sem,
    nr_sem, n_sem, nf_sem, f_sem, pipe_sem, pr_sem, p_sem, gx_sem, ga_sem, gb_sem, local_sem,
):
    p = lax.axis_index("pipe")
    t = lax.axis_index("tensor")
    dp = lax.axis_index("dp")
    z = lax.div(dp, RING)
    y = lax.rem(dp, RING)
    a = (1 - p) * z + p * y
    b = (1 - p) * y + p * z

    def dp_of(aa, bb):
        return (1 - p) * (RING * aa + bb) + p * (RING * bb + aa)

    def plus(i, o):
        return lax.rem(i + o, RING)

    def dev_x(o):
        return (p, plus(t, o), dp)

    def dev_a(o):
        return (p, t, dp_of(plus(a, o), b))

    def dev_b(o):
        return (p, t, dp_of(a, plus(b, o)))

    dev_p = (1 - p, t, dp)

    sends = []
    unfinished = {}

    def send(src, dst, recv_sem, device):
        copy = pltpu.make_async_remote_copy(
            src_ref=src, dst_ref=dst, send_sem=send_sem.at[len(sends)], recv_sem=recv_sem,
            device_id=device, device_id_type=MESH,
        )
        copy.start()
        sends.append(copy)
        unfinished[id(copy)] = copy
        return copy

    def finish(copies):
        for copy in copies:
            copy.wait_send()
            del unfinished[id(copy)]

    def arrived(dst, recv_sem):
        pltpu.make_async_remote_copy(
            src_ref=dst, dst_ref=dst, send_sem=send_sem.at[0], recv_sem=recv_sem,
            device_id=dev_p, device_id_type=MESH,
        ).wait_recv()

    class Gather:
        def __init__(self, view, sem, me, device):
            self.view, self.sem, self.me, self.device = view, sem, me, device

        def copy(self, owner, half, way):
            place = self.view(owner, half)
            send(place, place, self.sem(owner, half), self.device(way))

        def wait(self, owner, half):
            arrived(self.view(owner, half), self.sem(owner, half))

        def start(self):
            for half, way in ((0, 1), (1, 3), (1, 1), (0, 3)):
                self.copy(self.me, half, way)

        def forward(self):
            for half, origin, way in ((0, 3, 1), (1, 1, 3)):
                owner = plus(self.me, origin)
                self.wait(owner, half)
                self.copy(owner, half, way)

        def near(self):
            self.wait(plus(self.me, 3), 1)
            self.wait(plus(self.me, 1), 0)

        def far(self):
            self.wait(plus(self.me, 2), 0)
            self.wait(plus(self.me, 2), 1)

    class Scatter:
        def __init__(self, part, relay, recv, relay_sem, sem, me, device):
            self.part, self.relay, self.recv = part, relay, recv
            self.relay_sem, self.sem, self.me, self.device = relay_sem, sem, me, device
            self.copies = []

        def far(self):
            for half, way in ((0, 1), (1, 3)):
                self.copies.append(
                    send(self.part(plus(self.me, 2), half), self.relay(half), self.relay_sem(half),
                         self.device(way))
                )

        def direct(self, half):
            way, other = ((1, 3)[half], 1 - half)
            self.copies.append(
                send(self.part(plus(self.me, way), other), self.recv(half, other),
                     self.sem(half, other), self.device(way))
            )

        def onward(self, half):
            way = (1, 3)[half]
            arrived(self.relay(half), self.relay_sem(half))
            place = self.part(plus(self.me, way), half)
            place[...] = (place[...].astype(F32) + self.relay(half)[...].astype(F32)).astype(BF16)
            self.copies.append(
                send(place, self.recv(half, half), self.sem(half, half), self.device(way))
            )

        def wait(self):
            for way in range(2):
                for half in range(2):
                    arrived(self.recv(way, half), self.sem(way, half))

    barrier = pltpu.get_barrier_semaphore()
    partners = [f(o) for f in (dev_x, dev_a, dev_b) for o in ORDER] + [dev_p]
    partners += [(1 - p, t, dp_of(plus(a, o), b)) for o in ORDER]
    for device in partners:
        pl.semaphore_signal(barrier, inc=1, device_id=device, device_id_type=MESH)

    blocks = [(i, j) for i in range(RING) for j in range(RING)]

    def cols_of(j):
        return pl.ds(j * BLOCK, BLOCK)

    for i, j in blocks:
        pltpu.make_async_copy(
            top_hbm.at[:, at(dp_of(i, j), BLOCK)], up_own.at[0, i, :, cols_of(j)], local_sem.at[0]
        ).start()
    loads = [
        pltpu.make_async_copy(x_hbm, x_ref, local_sem.at[1]),
        pltpu.make_async_copy(q_hbm, q_ref, local_sem.at[2]),
        pltpu.make_async_copy(k_hbm, k_ref, local_sem.at[3]),
        pltpu.make_async_copy(v_hbm, v_ref, local_sem.at[4]),
        pltpu.make_async_copy(wo_ref, w_out.at[at(b, BLOCK), :], local_sem.at[5]),
        pltpu.make_async_copy(wq_ref, w_qkv.at[at(b, BLOCK), pl.ds(0, QCOLS)], local_sem.at[6]),
        pltpu.make_async_copy(
            wk_ref, w_qkv.at[at(b, BLOCK), pl.ds(QCOLS, KVCOLS)], local_sem.at[7]
        ),
        pltpu.make_async_copy(
            wv_ref, w_qkv.at[at(b, BLOCK), pl.ds(QCOLS + KVCOLS, KVCOLS)], local_sem.at[8]
        ),
    ]
    for copy in loads:
        copy.start()
    pltpu.make_async_copy(up_own.at[0], up_own.at[0], local_sem.at[0]).wait()
    pl.semaphore_wait(barrier, len(partners))

    rows_own = at(a, TOK)

    def half_rows(i, half, size):
        return pl.ds(pl.multiple_of(i * size + half * (size // 2), size // 2), size // 2)

    def slab(i):
        return pl.ds(pl.multiple_of(i * TOK + t * SUB, SUB), SUB)

    def part_rows(i, owner, h):
        return pl.ds(pl.multiple_of(i * TOK + owner * SUB + h * PART, PART), PART)

    def own_part(h):
        return pl.ds(h * PART, PART)

    def spread_nm(m):
        for o in ORDER:
            send(nm_own.at[m, plus(a, o)], nm_all.at[m, slab(a), :], nm_a_sem.at[m, a], dev_a(o))
        nm_all[m, slab(a), :] = nm_own[m, a]

    def spread_up(h):
        for o in ORDER:
            send(
                up_own.at[0, plus(a, o), own_part(h), :], up_all.at[0, part_rows(a, t, h), :],
                up_a_sem.at[0, a, h], dev_a(o),
            )
        up_all[0, part_rows(a, t, h), :] = up_own[0, a, own_part(h), :]

    def up_gather(m, step, h):
        i = plus(a, step)

        def view(owner, half):
            start = i * TOK + owner * SUB + h * PART + half * (PART // 2)
            return up_all.at[m, pl.ds(pl.multiple_of(start, PART // 2), PART // 2), :]

        return Gather(view, lambda owner, half: up_x_sem.at[m, i, h, owner, half], t, dev_x)

    def nm_gather(m, step):
        i = plus(a, step)

        def view(owner, half):
            start = i * TOK + owner * SUB + half * (SUB // 2)
            return nm_all.at[m, pl.ds(pl.multiple_of(start, SUB // 2), SUB // 2), :]

        return Gather(view, lambda owner, half: nm_x_sem.at[m, i, owner, half], t, dev_x)

    def d_gather(m, h):
        return Gather(
            lambda owner, half: d_all.at[m, owner, pl.ds(2 * half, 2), h],
            lambda owner, half: d_sem.at[m, h, owner, half], a, dev_a,
        )

    def row_gather(ref, sem, m):
        return Gather(
            lambda owner, half: ref.at[m, half_rows(owner, half, TOK), :],
            lambda owner, half: sem.at[m, owner, half], a, dev_a,
        )

    def weight_gather(ref, cols, index):
        return Gather(
            lambda owner, half: ref.at[half_rows(owner, half, BLOCK), cols],
            lambda owner, half: w_sem.at[index, owner, half], b, dev_b,
        )

    out_gather = weight_gather(w_out, slice(None), 0)
    qkv_gather = weight_gather(w_qkv, slice(None), 1)
    up_gathers = [
        {(step, h): up_gather(m, step, h) for step in range(RING) for h in range(2)}
        for m in range(2)
    ]
    nm_gathers = [[nm_gather(m, step) for step in range(RING)] for m in range(2)]
    d_gathers = [[d_gather(m, h) for h in range(2)] for m in range(2)]
    att_gathers = [row_gather(att_all, att_sem, m) for m in range(2)]

    def nm_start(m, step):
        i = plus(a, step)
        if step:
            arrived(nm_all.at[m, slab(i), :], nm_a_sem.at[m, i])
        nm_gathers[m][step].start()

    def norm(m):
        square = jnp.zeros((SUB, 1), F32)
        for f in range(16):
            x = x_ref[m, :, cols_of(f)].astype(F32)
            square = square + jnp.sum(x * x, axis=-1, keepdims=True)
        inv = lax.rsqrt(square * (1.0 / WIDTH) + EPS)
        inv_ref[m] = jnp.broadcast_to(inv, (SUB, HEAD))
        for i, j in blocks:
            feature = at(dp_of(i, j), BLOCK)
            x = x_ref[m, :, feature].astype(F32)
            nm_own[m, i, :, cols_of(j)] = (x * inv * gain_ref[:, feature]).astype(BF16)

    def forward(m):
        seg_row = jnp.broadcast_to(seg_ref[m : m + 1, :], (TOK, TOK)).astype(F32)
        seg_col = jnp.transpose(seg_row)
        row = lax.broadcasted_iota(jnp.int32, (TOK, TOK), 0)
        col = lax.broadcasted_iota(jnp.int32, (TOK, TOK), 1)
        allowed = (row <= col) & (seg_row == seg_col)
        bias = jnp.where(allowed, 0.0, -1e30).astype(F32)

        def group(g, carry):
            key = k_ref[m, :, at(g, HEAD)]
            value = v_ref[m, :, at(g, HEAD)]
            for h in range(RING):
                cols = at(g * RING + h, HEAD)
                scores = nt(key, q_ref[m, :, cols]) * SCALE + bias
                top = jnp.max(scores, axis=0, keepdims=True)
                raised = jnp.exp(scores - top)
                attention = raised * (1.0 / jnp.sum(raised, axis=0, keepdims=True))
                probs[m, g * RING + h] = attention
                att_all[m, rows_own, cols] = tn(attention.astype(BF16), value).astype(BF16)
            return carry

        lax.fori_loop(0, 2, group, 0)

    def grad_attn_rows(m, i, dst):
        def chunk(n, carry):
            cols = at(n, BLOCK)
            dst[:, cols] = nn(up_all[m, at(i, TOK), :], w_out[:, cols]).astype(BF16)
            return carry

        lax.fori_loop(0, RING, chunk, 0)

    def grad_attn_scatter(m):
        return Scatter(
            lambda dest, half: g_part.at[dest, pl.ds(half * 128, 128), :],
            lambda way: g_relay.at[way],
            lambda way, half: g_recv.at[way, pl.ds(half * 128, 128), :],
            lambda way: gr_sem.at[m, way],
            lambda way, half: g_sem.at[m, way, half],
            a, dev_a,
        )

    UNITS = ((0, 0), (1, 0), (3, 0), (2, 0), (2, 1), (1, 1), (3, 1), (0, 1))

    def up_start(m, units):
        for step, h in units:
            i = plus(a, step)
            if m or step:
                arrived(up_all.at[m, part_rows(i, t, h), :], up_a_sem.at[m, i, h])
            up_gathers[m][step, h].start()

    def up_forward(m, units):
        for unit in units:
            up_gathers[m][unit].forward()

    def grad_attn_partial(m):
        scatter = grad_attn_scatter(m)

        def rows(step):
            for h in range(2):
                up_gathers[m][step, h].near()
                up_gathers[m][step, h].far()
            i = plus(a, step)
            grad_attn_rows(m, i, g_part.at[i])

        rows(2)
        scatter.far()
        rows(1)
        scatter.direct(0)
        rows(3)
        scatter.direct(1)
        rows(0)
        return scatter

    def grad_attn_sum(m, scatter):
        scatter.wait()
        for n in range(RING):
            cols = cols_of(n)
            total = g_part[a, :, cols].astype(F32) + g_recv[0, :, cols].astype(F32)
            g_own[:, cols] = (total + g_recv[1, :, cols].astype(F32)).astype(BF16)

    def backward(m):
        def put(cols, value):
            d_all[m, a, :, :, :, cols] = value.astype(BF16).reshape(RING, 2, PART, HEAD)

        def group(g, carry):
            key = k_ref[m, :, at(g, HEAD)]
            value = v_ref[m, :, at(g, HEAD)]
            dk = jnp.zeros((TOK, HEAD), F32)
            dv = jnp.zeros((TOK, HEAD), F32)
            for h in range(RING):
                cols = at(g * RING + h, HEAD)
                grad = g_own[:, cols]
                attention = probs[m, g * RING + h]
                grad_probs = nt(value, grad)
                row_dot = jnp.sum(attention * grad_probs, axis=0, keepdims=True)
                score = (attention * (grad_probs - row_dot) * SCALE).astype(BF16)
                put(cols, tn(score, key))
                dk = dk + nn(score, q_ref[m, :, cols])
                dv = dv + nn(attention.astype(BF16), grad)
            put(pl.ds(pl.multiple_of(QCOLS + g * HEAD, HEAD), HEAD), dk)
            put(pl.ds(pl.multiple_of(QCOLS + KVCOLS + g * HEAD, HEAD), HEAD), dv)
            return carry

        lax.fori_loop(0, 2, group, 0)

    def grad_normed_rows(m, step, h):
        i = plus(a, step)

        def chunk(n, carry):
            cols = at(n, BLOCK)
            left = d_all[m, i, :, h].reshape(RING * PART, DCOLS)
            part = nt(left, w_qkv[at(n, BLOCK), :]).astype(BF16)
            for u in range(RING):
                n_part[u, i, h, :, cols] = part[u * PART : (u + 1) * PART, :]
            return carry

        lax.fori_loop(0, RING, chunk, 0)
        if step == 2:
            copies = [
                send(n_part.at[plus(t, 2), i, h], n_far.at[m, h], nf_sem.at[m, h], dev_x(2)),
                send(n_part.at[plus(t, 1), i, h], n_recv.at[m, 0, i, h], n_sem.at[m, 0, i, h, 0], dev_x(1)),
                send(n_part.at[plus(t, 3), i, h], n_recv.at[m, 1, i, h], n_sem.at[m, 1, i, h, 0], dev_x(3)),
            ]
            n_copies.extend(copies)
            return None
        scatter = Scatter(
            lambda dest, half: n_part.at[dest, i, h, pl.ds(half * 16, 16), :],
            lambda way: n_relay.at[m, way, i, h],
            lambda way, half: n_recv.at[m, way, i, h, pl.ds(half * 16, 16), :],
            lambda way: nr_sem.at[m, way, i, h],
            lambda way, half: n_sem.at[m, way, i, h, half],
            t, dev_x,
        )
        scatter.copies = n_copies
        scatter.far()
        scatter.direct(0)
        scatter.direct(1)
        return scatter

    def onward(scatter):
        scatter.onward(0)
        scatter.onward(1)

    def grad_normed_sum(m, step, h, scatter):
        i = plus(a, step)
        if step == 2:
            arrived(n_recv.at[m, 0, i, h], n_sem.at[m, 0, i, h, 0])
            arrived(n_recv.at[m, 1, i, h], n_sem.at[m, 1, i, h, 0])
            arrived(n_far.at[m, h], nf_sem.at[m, h])
        else:
            scatter.wait()
        for n in range(RING):
            cols = cols_of(n)
            total = n_part[t, i, h, :, cols].astype(F32) + n_recv[m, 0, i, h, :, cols].astype(F32)
            total = total + n_recv[m, 1, i, h, :, cols].astype(F32)
            if step == 2:
                total = total + n_far[m, h, :, cols].astype(F32)
            if step:
                n_sum[i, h, :, cols] = total.astype(BF16)
            else:
                f_recv[m, i, h, :, cols] = total.astype(BF16)
        if step:
            n_copies.append(
                send(n_sum.at[i, h], f_recv.at[m, a, h], f_sem.at[m, a, h], dev_a(step))
            )

    def grad_normed_back(m, h):
        for o in ORDER:
            arrived(f_recv.at[m, plus(a, o), h], f_sem.at[m, plus(a, o), h])

    def grad_input(m, h):
        rows = own_part(h)
        inv = inv_ref[m, rows, :][:, :1]
        total = jnp.zeros((PART, 1), F32)
        for i, j in blocks:
            feature = at(dp_of(i, j), BLOCK)
            unit = x_ref[m, rows, feature].astype(F32) * inv
            grad = f_recv[m, i, h, :, cols_of(j)].astype(F32)
            term = unit * grad
            total = total + jnp.sum(term * gain_ref[:, feature], axis=-1, keepdims=True)
            place = (pl.ds(i * 2 + j // 2, 1), cols_of(j % 2))
            gain_sum = jnp.sum(term, axis=0, keepdims=True)
            if m == 0 and h == 0:
                gain_mine[place] = gain_sum
            else:
                gain_mine[place] = gain_mine[place] + gain_sum
        mean = total * (1.0 / WIDTH)
        for i, j in blocks:
            feature = at(dp_of(i, j), BLOCK)
            unit = x_ref[m, rows, feature].astype(F32) * inv
            grad = f_recv[m, i, h, :, cols_of(j)].astype(F32)
            result = up_own[m, i, rows, cols_of(j)].astype(F32) + inv * (
                gain_ref[:, feature] * grad - unit * mean
            )
            if m == 0:
                pipe_src[j, rows, cols_of(i)] = result.astype(BF16)
            else:
                bottom_ref[rows, feature] = result.astype(BF16)

    def hand_down(h):
        rows = own_part(h)
        for o in (0,) + ORDER:
            j = plus(b, o)
            send(
                pipe_src.at[j, rows, :], up_all.at[1, part_rows(b, t, h), :],
                up_a_sem.at[1, b, h], (1 - p, t, dp_of(a, j)),
            )
        send(pipe_src.at[:, rows, :], up_own.at[1, :, rows, :], pipe_sem.at[h], dev_p)

    def weight_scatter(first, offset, width):
        return Scatter(
            lambda dest, half: p_part.at[dest, pl.ds(half * 128, 128), pl.ds(offset, width)],
            lambda way: p_relay.at[way, :, pl.ds(offset, width)],
            lambda way, half: p_recv.at[way, pl.ds(half * 128, 128), pl.ds(offset, width)],
            lambda way: pr_sem.at[first, way],
            lambda way, half: p_sem.at[first, way, half],
            b, dev_b,
        )

    def out_rows(step):
        j = plus(b, step)
        feature = at(j, BLOCK)

        def chunk(n, carry):
            cols = at(n, 512)
            total = tn(up_all[0, :, feature], att_all[0, :, cols])
            total = total + tn(up_all[1, :, feature], att_all[1, :, cols])
            place = pl.ds(pl.multiple_of(DCOLS + n * 512, 512), 512)
            p_part[j, :, place] = total.astype(BF16)
            return carry

        lax.fori_loop(0, QCOLS // 512, chunk, 0)

    def qkv_rows(m, step):
        j = plus(b, step)
        feature = at(j, BLOCK)

        def chunk(n, carry):
            cols = at(n, 512)
            total = tn(nm_all[m, :, feature], d_all[m, :, :, :, :, cols].reshape(GROUP, 512))
            if m == 0:
                p_early[j, :, cols] = total
            else:
                p_part[j, :, cols] = (p_early[j, :, cols] + total).astype(BF16)
            return carry

        lax.fori_loop(0, DCOLS // 512, chunk, 0)

    def summed(cols):
        total = p_part[b, :, cols].astype(F32) + p_recv[0, :, cols].astype(F32)
        return (total + p_recv[1, :, cols].astype(F32)).astype(BF16)

    n_copies = []
    out_scatter = weight_scatter(0, DCOLS, QCOLS)
    qkv_scatter = weight_scatter(1, 0, DCOLS)

    spread_up(0)
    spread_up(1)
    up_start(0, UNITS[:1])
    loads[4].wait()
    out_gather.start()
    loads[0].wait()
    norm(0)
    up_start(0, UNITS[1:])
    for copy in loads[1:4]:
        copy.wait()
    forward(0)
    att_gathers[0].start()
    spread_nm(0)
    for copy in loads[5:]:
        copy.wait()
    out_gather.forward()
    qkv_gather.start()
    up_forward(0, UNITS[:4])
    norm(1)
    spread_nm(1)
    forward(1)
    up_forward(0, UNITS[4:])
    att_gathers[0].forward()
    out_gather.near()
    out_gather.far()
    scatter = grad_attn_partial(0)
    g_copies = scatter.copies
    for step in (0, 1, 3, 2):
        nm_start(0, step)
    onward(scatter)
    qkv_gather.forward()
    grad_attn_sum(0, scatter)
    backward(0)

    def grad_normed(m):
        first, second = d_gathers[m]
        first.start()
        second.start()
        if m == 0:
            qkv_gather.near()
            qkv_gather.far()
        parts = {(0, 0): grad_normed_rows(m, 0, 0), (0, 1): grad_normed_rows(m, 0, 1)}
        first.forward()
        first.near()
        parts[1, 0] = grad_normed_rows(m, 1, 0)
        parts[3, 0] = grad_normed_rows(m, 3, 0)
        for step in (0, 1, 3, 2):
            nm_gathers[m][step].forward()
        onward(parts[0, 0])
        onward(parts[0, 1])
        second.forward()
        first.far()
        parts[2, 0] = grad_normed_rows(m, 2, 0)
        onward(parts[1, 0])
        onward(parts[3, 0])
        second.near()
        parts[1, 1] = grad_normed_rows(m, 1, 1)
        parts[3, 1] = grad_normed_rows(m, 3, 1)
        for step in (0, 1, 3, 2):
            grad_normed_sum(m, step, 0, parts[step, 0])
        second.far()
        parts[2, 1] = grad_normed_rows(m, 2, 1)
        onward(parts[1, 1])
        onward(parts[3, 1])
        return parts

    parts = grad_normed(0)
    grad_normed_back(0, 0)
    grad_input(0, 0)
    hand_down(0)
    for step in (0, 1, 3, 2):
        grad_normed_sum(0, step, 1, parts[step, 1])
    up_start(1, UNITS[:4])
    for gather in nm_gathers[0]:
        gather.near()
        gather.far()
    qkv_rows(0, 2)
    qkv_rows(0, 1)
    grad_normed_back(0, 1)
    grad_input(0, 1)
    hand_down(1)
    up_forward(1, UNITS[:4])
    att_gathers[1].start()
    qkv_rows(0, 3)
    qkv_rows(0, 0)

    up_start(1, UNITS[4:])
    up_forward(1, UNITS[4:])
    att_gathers[1].forward()
    finish(g_copies)
    scatter = grad_attn_partial(1)
    for step in (0, 1, 3, 2):
        nm_start(1, step)
    onward(scatter)
    for gather in att_gathers:
        gather.near()
        gather.far()
    out_rows(2)
    out_scatter.far()
    out_rows(1)
    out_scatter.direct(0)
    out_rows(3)
    out_scatter.direct(1)
    grad_attn_sum(1, scatter)
    backward(1)
    finish(n_copies)
    parts = grad_normed(1)
    onward(out_scatter)
    for gather in nm_gathers[1]:
        gather.near()
        gather.far()
    qkv_rows(1, 2)
    qkv_scatter.far()
    qkv_rows(1, 1)
    qkv_scatter.direct(0)
    for step in (0, 1, 3, 2):
        grad_normed_sum(1, step, 1, parts[step, 1])
    qkv_rows(1, 3)
    qkv_scatter.direct(1)
    for h in range(2):
        arrived(up_own.at[1, :, own_part(h), :], pipe_sem.at[h])
    grad_normed_back(1, 0)
    grad_input(1, 0)
    grad_normed_back(1, 1)
    grad_input(1, 1)

    gain_x[t] = gain_mine[...]
    for o in ORDER:
        send(gain_x.at[t], gain_x.at[t], gx_sem.at[t], dev_x(o))
    onward(qkv_scatter)
    qkv_rows(1, 0)
    for o in ORDER:
        arrived(gain_x.at[plus(t, o)], gx_sem.at[plus(t, o)])
    gain_a[a] = gain_x[0] + gain_x[1] + gain_x[2] + gain_x[3]
    for o in ORDER:
        send(gain_a.at[a], gain_a.at[a], ga_sem.at[a], dev_a(o))
    out_rows(0)
    out_scatter.wait()
    for n in range(4):
        go_ref[:, cols_of(n)] = summed(pl.ds(DCOLS + n * BLOCK, BLOCK))
    for o in ORDER:
        arrived(gain_a.at[plus(a, o)], ga_sem.at[plus(a, o)])
    gain_b[b] = gain_a[0] + gain_a[1] + gain_a[2] + gain_a[3]
    for o in ORDER:
        send(gain_b.at[b], gain_b.at[b], gb_sem.at[b], dev_b(o))
    qkv_scatter.wait()
    for n in range(4):
        gq_ref[:, cols_of(n)] = summed(cols_of(n))
    gk_ref[...] = summed(pl.ds(QCOLS, KVCOLS))
    gv_ref[...] = summed(pl.ds(QCOLS + KVCOLS, KVCOLS))
    for o in ORDER:
        arrived(gain_b.at[plus(b, o)], gb_sem.at[plus(b, o)])
    gain_mine[...] = gain_b[0] + gain_b[1] + gain_b[2] + gain_b[3]
    for i, j in blocks:
        gg_ref[:, at(dp_of(i, j), BLOCK)] = gain_mine[pl.ds(i * 2 + j // 2, 1), cols_of(j % 2)]

    finish(list(unfinished.values()))


def hand_out(*refs):
    for src, dst in zip(refs[:6], refs[6:]):
        dst[...] = src[...]


def local(x_saved, grad_top, query, key, value, segment, w_query, key_weight, value_weight, w_out, gain):
    vmem = pl.BlockSpec(memory_space=pltpu.VMEM)
    hbm = pl.BlockSpec(memory_space=pl.ANY)
    dma = pltpu.SemaphoreType.DMA
    outs = pl.pallas_call(
        kernel,
        out_shape=(
            jax.ShapeDtypeStruct((SUB, WIDTH), BF16),
            jax.ShapeDtypeStruct((BLOCK, QCOLS), BF16),
            jax.ShapeDtypeStruct((BLOCK, KVCOLS), BF16),
            jax.ShapeDtypeStruct((BLOCK, KVCOLS), BF16),
            jax.ShapeDtypeStruct((BLOCK, QCOLS), BF16),
            jax.ShapeDtypeStruct((1, WIDTH), F32),
        ),
        in_specs=[hbm] * 5 + [vmem] * 2 + [hbm] * 4,
        out_specs=(vmem,) * 6,
        scratch_shapes=[
            pltpu.VMEM((2, SUB, WIDTH), BF16),
            pltpu.VMEM((2, TOK, QCOLS), BF16),
            pltpu.VMEM((2, TOK, KVCOLS), BF16),
            pltpu.VMEM((2, TOK, KVCOLS), BF16),
            pltpu.VMEM((2, RING, SUB, GROUP), BF16),
            pltpu.VMEM((2, RING, SUB, GROUP), BF16),
            pltpu.VMEM((2, GROUP, GROUP), BF16),
            pltpu.VMEM((2, GROUP, GROUP), BF16),
            pltpu.VMEM((GROUP, QCOLS), BF16),
            pltpu.VMEM((GROUP, DCOLS), BF16),
            pltpu.VMEM((2, RING, RING, 2, PART, DCOLS), BF16),
            pltpu.VMEM((2, GROUP, QCOLS), BF16),
            pltpu.VMEM((RING, TOK, QCOLS), BF16),
            pltpu.VMEM((2, TOK // 2, QCOLS), BF16),
            pltpu.VMEM((2, TOK, QCOLS), BF16),
            pltpu.VMEM((TOK, QCOLS), BF16),
            pltpu.VMEM((2, 8, TOK, TOK), F32),
            pltpu.VMEM((RING, RING, 2, PART, GROUP), BF16),
            pltpu.VMEM((2, 2, RING, 2, PART // 2, GROUP), BF16),
            pltpu.VMEM((2, 2, RING, 2, PART, GROUP), BF16),
            pltpu.VMEM((2, 2, PART, GROUP), BF16),
            pltpu.VMEM((RING, 2, PART, GROUP), BF16),
            pltpu.VMEM((2, RING, 2, PART, GROUP), BF16),
            pltpu.VMEM((RING, SUB, GROUP), BF16),
            pltpu.VMEM((RING, BLOCK, DCOLS), F32),
            pltpu.VMEM((RING, BLOCK, ALLCOLS), BF16),
            pltpu.VMEM((2, BLOCK // 2, ALLCOLS), BF16),
            pltpu.VMEM((2, BLOCK, ALLCOLS), BF16),
            pltpu.VMEM((2, SUB, HEAD), F32),
            pltpu.VMEM((8, 512), F32),
            pltpu.VMEM((RING, 8, 512), F32),
            pltpu.VMEM((RING, 8, 512), F32),
            pltpu.VMEM((RING, 8, 512), F32),
            dma((400,)),
            dma((2, RING, 2)),
            dma((2, RING, 2, RING, 2)),
            dma((2, RING)),
            dma((2, RING, RING, 2)),
            dma((2, RING, 2)),
            dma((2, 2)),
            dma((2, 2, 2)),
            dma((2, 2, RING, 2)),
            dma((2, RING, 2)),
            dma((2, 2, RING, 2)),
            dma((2, 2, RING, 2, 2)),
            dma((2, 2)),
            dma((2, RING, 2)),
            dma((2,)),
            dma((2, 2)),
            dma((2, 2, 2)),
            dma((RING,)),
            dma((RING,)),
            dma((RING,)),
            dma((9,)),
        ],
        compiler_params=pltpu.CompilerParams(
            collective_id=0, has_side_effects=True, vmem_limit_bytes=63 * 2**20
        ),
        cost_estimate=pl.CostEstimate(flops=23 * 10**9, bytes_accessed=8 * 10**6, transcendentals=10**6),
        name="relay_backward",
    )(
        x_saved[0, 0], grad_top[0, 0], query[0, 0], key[0, 0], value[0, 0], segment[0, 0], gain,
        w_query[0], key_weight[0], value_weight[0], w_out[0],
    )
    bottom, gq, gk, gv, go, gg = pl.pallas_call(
        hand_out,
        out_shape=tuple(jax.ShapeDtypeStruct(out.shape, out.dtype) for out in outs),
        in_specs=[vmem] * 6,
        out_specs=(vmem,) * 6,
        name="hand_out",
    )(*outs)
    return (bottom[None, None], gq[None], gk[None], gv[None], go[None], gg)


def solution(mesh):
    in_specs = (
        P("pipe", "dp", None, "tensor", None),
        P("pipe", "dp", "tensor", None),
        P("pipe", "dp", None, None, "tensor"),
        P("pipe", "dp", None, None, "tensor"),
        P("pipe", "dp", None, None, "tensor"),
        P("pipe", "dp", None, None),
        P("pipe", "dp", "tensor"),
        P("pipe", "dp", "tensor"),
        P("pipe", "dp", "tensor"),
        P("pipe", "dp", "tensor"),
        P("pipe", None),
    )
    out_specs = (
        P("pipe", "dp", "tensor", None),
        P("pipe", "dp", "tensor"),
        P("pipe", "dp", "tensor"),
        P("pipe", "dp", "tensor"),
        P("pipe", "dp", "tensor"),
        P("pipe", None),
    )
    return jax.shard_map(local, mesh=mesh, in_specs=in_specs, out_specs=out_specs, check_vma=False)
```

```python
import functools
import math

import jax
import jax.numpy as jnp
from jax import lax
from jax.experimental import pallas as pl
from jax.experimental.pallas import tpu as pltpu
from jax.sharding import PartitionSpec as P

BF16 = jnp.bfloat16
F32 = jnp.float32
MESH = pl.DeviceIdType.MESH
HEAD = 128
EPS = 1e-05
RING = 4
TOK = 256
SUB = 64
WIDTH = 4096
GROUP = 1024
BLOCK = 256
QCOLS = 1024
KVCOLS = 256
DCOLS = QCOLS + 2 * KVCOLS
ALLCOLS = DCOLS + QCOLS
SCALE = 1.0 / math.sqrt(HEAD)
ORDER = (1, 3, 2)
PART = 32


def nn(left, right):
    return lax.dot_general(left, right, (((1,), (0,)), ((), ())), preferred_element_type=F32)


def nt(left, right):
    return lax.dot_general(left, right, (((1,), (1,)), ((), ())), preferred_element_type=F32)


def tn(left, right):
    return lax.dot_general(left, right, (((0,), (0,)), ((), ())), preferred_element_type=F32)


def at(index, size):
    return pl.ds(pl.multiple_of(index * size, size), size)


def kernel(
    x_hbm, top_hbm, q_hbm, k_hbm, v_hbm, seg_ref, gain_ref, wq_ref, wk_ref, wv_ref, wo_ref,
    bottom_ref, gq_ref, gk_ref, gv_ref, go_ref, gg_ref,
    x_ref, q_ref, k_ref, v_ref,
    up_own, nm_own, up_all, nm_all, w_out, w_qkv, d_all, att_all,
    g_part, g_relay, g_recv, g_own, probs,
    n_part, n_relay, n_recv, n_far, n_sum, f_recv, pipe_src, p_early, p_part, p_relay, p_recv, inv_ref,
    gain_mine, gain_x, gain_a, gain_b,
    send_sem, up_a_sem, up_x_sem, nm_a_sem, nm_x_sem, w_sem, gr_sem, g_sem, d_sem, att_sem,
    nr_sem, n_sem, nf_sem, f_sem, pipe_sem, pr_sem, p_sem, gx_sem, ga_sem, gb_sem, local_sem,
):
    p = lax.axis_index("pipe")
    t = lax.axis_index("tensor")
    dp = lax.axis_index("dp")
    z = lax.div(dp, RING)
    y = lax.rem(dp, RING)
    a = (1 - p) * z + p * y
    b = (1 - p) * y + p * z

    def dp_of(aa, bb):
        return (1 - p) * (RING * aa + bb) + p * (RING * bb + aa)

    def plus(i, o):
        return lax.rem(i + o, RING)

    def dev_x(o):
        return (p, plus(t, o), dp)

    def dev_a(o):
        return (p, t, dp_of(plus(a, o), b))

    def dev_b(o):
        return (p, t, dp_of(a, plus(b, o)))

    dev_p = (1 - p, t, dp)

    sends = []
    unfinished = {}

    def send(src, dst, recv_sem, device):
        copy = pltpu.make_async_remote_copy(
            src_ref=src, dst_ref=dst, send_sem=send_sem.at[len(sends)], recv_sem=recv_sem,
            device_id=device, device_id_type=MESH,
        )
        copy.start()
        sends.append(copy)
        unfinished[id(copy)] = copy
        return copy

    def finish(copies):
        for copy in copies:
            copy.wait_send()
            del unfinished[id(copy)]

    def arrived(dst, recv_sem):
        pltpu.make_async_remote_copy(
            src_ref=dst, dst_ref=dst, send_sem=send_sem.at[0], recv_sem=recv_sem,
            device_id=dev_p, device_id_type=MESH,
        ).wait_recv()

    class Gather:
        def __init__(self, view, sem, me, device):
            self.view, self.sem, self.me, self.device = view, sem, me, device

        def copy(self, owner, half, way):
            place = self.view(owner, half)
            send(place, place, self.sem(owner, half), self.device(way))

        def wait(self, owner, half):
            arrived(self.view(owner, half), self.sem(owner, half))

        def start(self):
            for half, way in ((0, 1), (1, 3), (1, 1), (0, 3)):
                self.copy(self.me, half, way)

        def forward(self):
            for half, origin, way in ((0, 3, 1), (1, 1, 3)):
                owner = plus(self.me, origin)
                self.wait(owner, half)
                self.copy(owner, half, way)

        def near(self):
            self.wait(plus(self.me, 3), 1)
            self.wait(plus(self.me, 1), 0)

        def far(self):
            self.wait(plus(self.me, 2), 0)
            self.wait(plus(self.me, 2), 1)

    class Scatter:
        def __init__(self, part, relay, recv, relay_sem, sem, me, device):
            self.part, self.relay, self.recv = part, relay, recv
            self.relay_sem, self.sem, self.me, self.device = relay_sem, sem, me, device
            self.copies = []

        def far(self):
            for half, way in ((0, 1), (1, 3)):
                self.copies.append(
                    send(self.part(plus(self.me, 2), half), self.relay(half), self.relay_sem(half),
                         self.device(way))
                )

        def direct(self, half):
            way, other = ((1, 3)[half], 1 - half)
            self.copies.append(
                send(self.part(plus(self.me, way), other), self.recv(half, other),
                     self.sem(half, other), self.device(way))
            )

        def onward(self, half):
            way = (1, 3)[half]
            arrived(self.relay(half), self.relay_sem(half))
            place = self.part(plus(self.me, way), half)
            place[...] = (place[...].astype(F32) + self.relay(half)[...].astype(F32)).astype(BF16)
            self.copies.append(
                send(place, self.recv(half, half), self.sem(half, half), self.device(way))
            )

        def wait(self):
            for way in range(2):
                for half in range(2):
                    arrived(self.recv(way, half), self.sem(way, half))

    barrier = pltpu.get_barrier_semaphore()
    partners = [f(o) for f in (dev_x, dev_a, dev_b) for o in ORDER] + [dev_p]
    partners += [(1 - p, t, dp_of(plus(a, o), b)) for o in ORDER]
    for device in partners:
        pl.semaphore_signal(barrier, inc=1, device_id=device, device_id_type=MESH)

    blocks = [(i, j) for i in range(RING) for j in range(RING)]

    def cols_of(j):
        return pl.ds(j * BLOCK, BLOCK)

    for i, j in blocks:
        pltpu.make_async_copy(
            top_hbm.at[:, at(dp_of(i, j), BLOCK)], up_own.at[0, i, :, cols_of(j)], local_sem.at[0]
        ).start()
    loads = [
        pltpu.make_async_copy(x_hbm, x_ref, local_sem.at[1]),
        pltpu.make_async_copy(q_hbm, q_ref, local_sem.at[2]),
        pltpu.make_async_copy(k_hbm, k_ref, local_sem.at[3]),
        pltpu.make_async_copy(v_hbm, v_ref, local_sem.at[4]),
        pltpu.make_async_copy(wo_ref, w_out.at[at(b, BLOCK), :], local_sem.at[5]),
        pltpu.make_async_copy(wq_ref, w_qkv.at[at(b, BLOCK), pl.ds(0, QCOLS)], local_sem.at[6]),
        pltpu.make_async_copy(
            wk_ref, w_qkv.at[at(b, BLOCK), pl.ds(QCOLS, KVCOLS)], local_sem.at[7]
        ),
        pltpu.make_async_copy(
            wv_ref, w_qkv.at[at(b, BLOCK), pl.ds(QCOLS + KVCOLS, KVCOLS)], local_sem.at[8]
        ),
    ]
    for copy in loads:
        copy.start()
    pltpu.make_async_copy(up_own.at[0], up_own.at[0], local_sem.at[0]).wait()
    pl.semaphore_wait(barrier, len(partners))

    rows_own = at(a, TOK)

    def half_rows(i, half, size):
        return pl.ds(pl.multiple_of(i * size + half * (size // 2), size // 2), size // 2)

    def slab(i):
        return pl.ds(pl.multiple_of(i * TOK + t * SUB, SUB), SUB)

    def part_rows(i, owner, h):
        return pl.ds(pl.multiple_of(i * TOK + owner * SUB + h * PART, PART), PART)

    def own_part(h):
        return pl.ds(h * PART, PART)

    def spread_nm(m):
        for o in ORDER:
            send(nm_own.at[m, plus(a, o)], nm_all.at[m, slab(a), :], nm_a_sem.at[m, a], dev_a(o))
        nm_all[m, slab(a), :] = nm_own[m, a]

    def spread_up(h):
        for o in ORDER:
            send(
                up_own.at[0, plus(a, o), own_part(h), :], up_all.at[0, part_rows(a, t, h), :],
                up_a_sem.at[0, a, h], dev_a(o),
            )
        up_all[0, part_rows(a, t, h), :] = up_own[0, a, own_part(h), :]

    def up_gather(m, step, h):
        i = plus(a, step)

        def view(owner, half):
            start = i * TOK + owner * SUB + h * PART + half * (PART // 2)
            return up_all.at[m, pl.ds(pl.multiple_of(start, PART // 2), PART // 2), :]

        return Gather(view, lambda owner, half: up_x_sem.at[m, i, h, owner, half], t, dev_x)

    def nm_gather(m, step):
        i = plus(a, step)

        def view(owner, half):
            start = i * TOK + owner * SUB + half * (SUB // 2)
            return nm_all.at[m, pl.ds(pl.multiple_of(start, SUB // 2), SUB // 2), :]

        return Gather(view, lambda owner, half: nm_x_sem.at[m, i, owner, half], t, dev_x)

    def d_gather(m, h):
        return Gather(
            lambda owner, half: d_all.at[m, owner, pl.ds(2 * half, 2), h],
            lambda owner, half: d_sem.at[m, h, owner, half], a, dev_a,
        )

    def row_gather(ref, sem, m):
        return Gather(
            lambda owner, half: ref.at[m, half_rows(owner, half, TOK), :],
            lambda owner, half: sem.at[m, owner, half], a, dev_a,
        )

    def weight_gather(ref, cols, index):
        return Gather(
            lambda owner, half: ref.at[half_rows(owner, half, BLOCK), cols],
            lambda owner, half: w_sem.at[index, owner, half], b, dev_b,
        )

    out_gather = weight_gather(w_out, slice(None), 0)
    qkv_gather = weight_gather(w_qkv, slice(None), 1)
    up_gathers = [
        {(step, h): up_gather(m, step, h) for step in range(RING) for h in range(2)}
        for m in range(2)
    ]
    nm_gathers = [[nm_gather(m, step) for step in range(RING)] for m in range(2)]
    d_gathers = [[d_gather(m, h) for h in range(2)] for m in range(2)]
    att_gathers = [row_gather(att_all, att_sem, m) for m in range(2)]

    def nm_start(m, step):
        i = plus(a, step)
        if step:
            arrived(nm_all.at[m, slab(i), :], nm_a_sem.at[m, i])
        nm_gathers[m][step].start()

    def norm(m):
        square = jnp.zeros((SUB, 1), F32)
        for f in range(16):
            x = x_ref[m, :, cols_of(f)].astype(F32)
            square = square + jnp.sum(x * x, axis=-1, keepdims=True)
        inv = lax.rsqrt(square * (1.0 / WIDTH) + EPS)
        inv_ref[m] = jnp.broadcast_to(inv, (SUB, HEAD))
        for i, j in blocks:
            feature = at(dp_of(i, j), BLOCK)
            x = x_ref[m, :, feature].astype(F32)
            nm_own[m, i, :, cols_of(j)] = (x * inv * gain_ref[:, feature]).astype(BF16)

    def forward(m):
        seg_row = jnp.broadcast_to(seg_ref[m : m + 1, :], (TOK, TOK)).astype(F32)
        seg_col = jnp.transpose(seg_row)
        row = lax.broadcasted_iota(jnp.int32, (TOK, TOK), 0)
        col = lax.broadcasted_iota(jnp.int32, (TOK, TOK), 1)
        allowed = (row <= col) & (seg_row == seg_col)
        bias = jnp.where(allowed, 0.0, -1e30).astype(F32)

        def group(g, carry):
            key = k_ref[m, :, at(g, HEAD)]
            value = v_ref[m, :, at(g, HEAD)]
            for h in range(RING):
                cols = at(g * RING + h, HEAD)
                scores = nt(key, q_ref[m, :, cols]) * SCALE + bias
                top = jnp.max(scores, axis=0, keepdims=True)
                raised = jnp.exp(scores - top)
                attention = raised * (1.0 / jnp.sum(raised, axis=0, keepdims=True))
                probs[m, g * RING + h] = attention
                att_all[m, rows_own, cols] = tn(attention.astype(BF16), value).astype(BF16)
            return carry

        lax.fori_loop(0, 2, group, 0)

    def grad_attn_rows(m, i, dst):
        def chunk(n, carry):
            cols = at(n, BLOCK)
            dst[:, cols] = nn(up_all[m, at(i, TOK), :], w_out[:, cols]).astype(BF16)
            return carry

        lax.fori_loop(0, RING, chunk, 0)

    def grad_attn_scatter(m):
        return Scatter(
            lambda dest, half: g_part.at[dest, pl.ds(half * 128, 128), :],
            lambda way: g_relay.at[way],
            lambda way, half: g_recv.at[way, pl.ds(half * 128, 128), :],
            lambda way: gr_sem.at[m, way],
            lambda way, half: g_sem.at[m, way, half],
            a, dev_a,
        )

    UNITS = ((0, 0), (1, 0), (3, 0), (2, 0), (2, 1), (1, 1), (3, 1), (0, 1))

    def up_start(m, units):
        for step, h in units:
            i = plus(a, step)
            if m or step:
                arrived(up_all.at[m, part_rows(i, t, h), :], up_a_sem.at[m, i, h])
            up_gathers[m][step, h].start()

    def up_forward(m, units):
        for unit in units:
            up_gathers[m][unit].forward()

    def grad_attn_partial(m):
        scatter = grad_attn_scatter(m)

        def rows(step):
            for h in range(2):
                up_gathers[m][step, h].near()
                up_gathers[m][step, h].far()
            i = plus(a, step)
            grad_attn_rows(m, i, g_part.at[i])

        rows(2)
        scatter.far()
        rows(1)
        scatter.direct(0)
        rows(3)
        scatter.direct(1)
        rows(0)
        return scatter

    def grad_attn_sum(m, scatter):
        scatter.wait()
        for n in range(RING):
            cols = cols_of(n)
            total = g_part[a, :, cols].astype(F32) + g_recv[0, :, cols].astype(F32)
            g_own[:, cols] = (total + g_recv[1, :, cols].astype(F32)).astype(BF16)

    def backward(m):
        def put(cols, value):
            d_all[m, a, :, :, :, cols] = value.astype(BF16).reshape(RING, 2, PART, HEAD)

        def group(g, carry):
            key = k_ref[m, :, at(g, HEAD)]
            value = v_ref[m, :, at(g, HEAD)]
            dk = jnp.zeros((TOK, HEAD), F32)
            dv = jnp.zeros((TOK, HEAD), F32)
            for h in range(RING):
                cols = at(g * RING + h, HEAD)
                grad = g_own[:, cols]
                attention = probs[m, g * RING + h]
                grad_probs = nt(value, grad)
                row_dot = jnp.sum(attention * grad_probs, axis=0, keepdims=True)
                score = (attention * (grad_probs - row_dot) * SCALE).astype(BF16)
                put(cols, tn(score, key))
                dk = dk + nn(score, q_ref[m, :, cols])
                dv = dv + nn(attention.astype(BF16), grad)
            put(pl.ds(pl.multiple_of(QCOLS + g * HEAD, HEAD), HEAD), dk)
            put(pl.ds(pl.multiple_of(QCOLS + KVCOLS + g * HEAD, HEAD), HEAD), dv)
            return carry

        lax.fori_loop(0, 2, group, 0)

    def grad_normed_rows(m, step, h):
        i = plus(a, step)

        def chunk(n, carry):
            cols = at(n, BLOCK)
            left = d_all[m, i, :, h].reshape(RING * PART, DCOLS)
            part = nt(left, w_qkv[at(n, BLOCK), :]).astype(BF16)
            for u in range(RING):
                n_part[u, i, h, :, cols] = part[u * PART : (u + 1) * PART, :]
            return carry

        lax.fori_loop(0, RING, chunk, 0)
        if step == 2:
            copies = [
                send(n_part.at[plus(t, 2), i, h], n_far.at[m, h], nf_sem.at[m, h], dev_x(2)),
                send(n_part.at[plus(t, 1), i, h], n_recv.at[m, 0, i, h], n_sem.at[m, 0, i, h, 0], dev_x(1)),
                send(n_part.at[plus(t, 3), i, h], n_recv.at[m, 1, i, h], n_sem.at[m, 1, i, h, 0], dev_x(3)),
            ]
            n_copies.extend(copies)
            return None
        scatter = Scatter(
            lambda dest, half: n_part.at[dest, i, h, pl.ds(half * 16, 16), :],
            lambda way: n_relay.at[m, way, i, h],
            lambda way, half: n_recv.at[m, way, i, h, pl.ds(half * 16, 16), :],
            lambda way: nr_sem.at[m, way, i, h],
            lambda way, half: n_sem.at[m, way, i, h, half],
            t, dev_x,
        )
        scatter.copies = n_copies
        scatter.far()
        scatter.direct(0)
        scatter.direct(1)
        return scatter

    def onward(scatter):
        scatter.onward(0)
        scatter.onward(1)

    def grad_normed_sum(m, step, h, scatter):
        i = plus(a, step)
        if step == 2:
            arrived(n_recv.at[m, 0, i, h], n_sem.at[m, 0, i, h, 0])
            arrived(n_recv.at[m, 1, i, h], n_sem.at[m, 1, i, h, 0])
            arrived(n_far.at[m, h], nf_sem.at[m, h])
        else:
            scatter.wait()
        for n in range(RING):
            cols = cols_of(n)
            total = n_part[t, i, h, :, cols].astype(F32) + n_recv[m, 0, i, h, :, cols].astype(F32)
            total = total + n_recv[m, 1, i, h, :, cols].astype(F32)
            if step == 2:
                total = total + n_far[m, h, :, cols].astype(F32)
            if step:
                n_sum[i, h, :, cols] = total.astype(BF16)
            else:
                f_recv[m, i, h, :, cols] = total.astype(BF16)
        if step:
            n_copies.append(
                send(n_sum.at[i, h], f_recv.at[m, a, h], f_sem.at[m, a, h], dev_a(step))
            )

    def grad_normed_back(m, h):
        for o in ORDER:
            arrived(f_recv.at[m, plus(a, o), h], f_sem.at[m, plus(a, o), h])

    def grad_input(m, h):
        rows = own_part(h)
        inv = inv_ref[m, rows, :][:, :1]
        total = jnp.zeros((PART, 1), F32)
        for i, j in blocks:
            feature = at(dp_of(i, j), BLOCK)
            unit = x_ref[m, rows, feature].astype(F32) * inv
            grad = f_recv[m, i, h, :, cols_of(j)].astype(F32)
            term = unit * grad
            total = total + jnp.sum(term * gain_ref[:, feature], axis=-1, keepdims=True)
            place = (pl.ds(i * 2 + j // 2, 1), cols_of(j % 2))
            gain_sum = jnp.sum(term, axis=0, keepdims=True)
            if m == 0 and h == 0:
                gain_mine[place] = gain_sum
            else:
                gain_mine[place] = gain_mine[place] + gain_sum
        mean = total * (1.0 / WIDTH)
        for i, j in blocks:
            feature = at(dp_of(i, j), BLOCK)
            unit = x_ref[m, rows, feature].astype(F32) * inv
            grad = f_recv[m, i, h, :, cols_of(j)].astype(F32)
            result = up_own[m, i, rows, cols_of(j)].astype(F32) + inv * (
                gain_ref[:, feature] * grad - unit * mean
            )
            if m == 0:
                pipe_src[j, rows, cols_of(i)] = result.astype(BF16)
            else:
                bottom_ref[rows, feature] = result.astype(BF16)

    def hand_down(h):
        rows = own_part(h)
        for o in (0,) + ORDER:
            j = plus(b, o)
            send(
                pipe_src.at[j, rows, :], up_all.at[1, part_rows(b, t, h), :],
                up_a_sem.at[1, b, h], (1 - p, t, dp_of(a, j)),
            )
        send(pipe_src.at[:, rows, :], up_own.at[1, :, rows, :], pipe_sem.at[h], dev_p)

    def weight_scatter(first, offset, width):
        return Scatter(
            lambda dest, half: p_part.at[dest, pl.ds(half * 128, 128), pl.ds(offset, width)],
            lambda way: p_relay.at[way, :, pl.ds(offset, width)],
            lambda way, half: p_recv.at[way, pl.ds(half * 128, 128), pl.ds(offset, width)],
            lambda way: pr_sem.at[first, way],
            lambda way, half: p_sem.at[first, way, half],
            b, dev_b,
        )

    def out_rows(step):
        j = plus(b, step)
        feature = at(j, BLOCK)

        def chunk(n, carry):
            cols = at(n, 512)
            total = tn(up_all[0, :, feature], att_all[0, :, cols])
            total = total + tn(up_all[1, :, feature], att_all[1, :, cols])
            place = pl.ds(pl.multiple_of(DCOLS + n * 512, 512), 512)
            p_part[j, :, place] = total.astype(BF16)
            return carry

        lax.fori_loop(0, QCOLS // 512, chunk, 0)

    def qkv_rows(m, step):
        j = plus(b, step)
        feature = at(j, BLOCK)

        def chunk(n, carry):
            cols = at(n, 512)
            total = tn(nm_all[m, :, feature], d_all[m, :, :, :, :, cols].reshape(GROUP, 512))
            if m == 0:
                p_early[j, :, cols] = total
            else:
                p_part[j, :, cols] = (p_early[j, :, cols] + total).astype(BF16)
            return carry

        lax.fori_loop(0, DCOLS // 512, chunk, 0)

    def summed(cols):
        total = p_part[b, :, cols].astype(F32) + p_recv[0, :, cols].astype(F32)
        return (total + p_recv[1, :, cols].astype(F32)).astype(BF16)

    n_copies = []
    out_scatter = weight_scatter(0, DCOLS, QCOLS)
    qkv_scatter = weight_scatter(1, 0, DCOLS)

    spread_up(0)
    spread_up(1)
    up_start(0, UNITS[:1])
    loads[4].wait()
    out_gather.start()
    loads[0].wait()
    norm(0)
    up_start(0, UNITS[1:])
    for copy in loads[1:4]:
        copy.wait()
    forward(0)
    att_gathers[0].start()
    spread_nm(0)
    for copy in loads[5:]:
        copy.wait()
    out_gather.forward()
    qkv_gather.start()
    up_forward(0, UNITS[:4])
    norm(1)
    spread_nm(1)
    forward(1)
    up_forward(0, UNITS[4:])
    att_gathers[0].forward()
    out_gather.near()
    out_gather.far()
    scatter = grad_attn_partial(0)
    g_copies = scatter.copies
    for step in (0, 1, 3, 2):
        nm_start(0, step)
    onward(scatter)
    qkv_gather.forward()
    grad_attn_sum(0, scatter)
    backward(0)

    def grad_normed(m):
        first, second = d_gathers[m]
        first.start()
        second.start()
        if m == 0:
            qkv_gather.near()
            qkv_gather.far()
        parts = {(0, 0): grad_normed_rows(m, 0, 0), (0, 1): grad_normed_rows(m, 0, 1)}
        first.forward()
        for step in (0, 1, 3, 2):
            nm_gathers[m][step].forward()
        first.near()
        parts[1, 0] = grad_normed_rows(m, 1, 0)
        parts[3, 0] = grad_normed_rows(m, 3, 0)
        onward(parts[0, 0])
        onward(parts[0, 1])
        second.forward()
        first.far()
        parts[2, 0] = grad_normed_rows(m, 2, 0)
        onward(parts[1, 0])
        onward(parts[3, 0])
        second.near()
        parts[1, 1] = grad_normed_rows(m, 1, 1)
        parts[3, 1] = grad_normed_rows(m, 3, 1)
        for step in (0, 1, 3, 2):
            grad_normed_sum(m, step, 0, parts[step, 0])
        second.far()
        parts[2, 1] = grad_normed_rows(m, 2, 1)
        onward(parts[1, 1])
        onward(parts[3, 1])
        return parts

    parts = grad_normed(0)
    grad_normed_back(0, 0)
    grad_input(0, 0)
    hand_down(0)
    for step in (0, 1, 3, 2):
        grad_normed_sum(0, step, 1, parts[step, 1])
    up_start(1, UNITS[:4])
    for gather in nm_gathers[0]:
        gather.near()
        gather.far()
    qkv_rows(0, 2)
    qkv_rows(0, 1)
    grad_normed_back(0, 1)
    grad_input(0, 1)
    hand_down(1)
    up_forward(1, UNITS[:4])
    att_gathers[1].start()
    qkv_rows(0, 3)
    qkv_rows(0, 0)

    up_start(1, UNITS[4:])
    up_forward(1, UNITS[4:])
    att_gathers[1].forward()
    finish(g_copies)
    scatter = grad_attn_partial(1)
    for step in (0, 1, 3, 2):
        nm_start(1, step)
    onward(scatter)
    for gather in att_gathers:
        gather.near()
        gather.far()
    out_rows(2)
    out_scatter.far()
    out_rows(1)
    out_scatter.direct(0)
    out_rows(3)
    out_scatter.direct(1)
    grad_attn_sum(1, scatter)
    backward(1)
    finish(n_copies)
    parts = grad_normed(1)
    onward(out_scatter)
    for gather in nm_gathers[1]:
        gather.near()
        gather.far()
    qkv_rows(1, 2)
    qkv_scatter.far()
    qkv_rows(1, 1)
    qkv_scatter.direct(0)
    for step in (0, 1, 3, 2):
        grad_normed_sum(1, step, 1, parts[step, 1])
    qkv_rows(1, 3)
    qkv_scatter.direct(1)
    for h in range(2):
        arrived(up_own.at[1, :, own_part(h), :], pipe_sem.at[h])
    grad_normed_back(1, 0)
    grad_input(1, 0)
    grad_normed_back(1, 1)
    grad_input(1, 1)

    gain_x[t] = gain_mine[...]
    for o in ORDER:
        send(gain_x.at[t], gain_x.at[t], gx_sem.at[t], dev_x(o))
    onward(qkv_scatter)
    qkv_rows(1, 0)
    for o in ORDER:
        arrived(gain_x.at[plus(t, o)], gx_sem.at[plus(t, o)])
    gain_a[a] = gain_x[0] + gain_x[1] + gain_x[2] + gain_x[3]
    for o in ORDER:
        send(gain_a.at[a], gain_a.at[a], ga_sem.at[a], dev_a(o))
    out_rows(0)
    out_scatter.wait()
    for n in range(4):
        go_ref[:, cols_of(n)] = summed(pl.ds(DCOLS + n * BLOCK, BLOCK))
    for o in ORDER:
        arrived(gain_a.at[plus(a, o)], ga_sem.at[plus(a, o)])
    gain_b[b] = gain_a[0] + gain_a[1] + gain_a[2] + gain_a[3]
    for o in ORDER:
        send(gain_b.at[b], gain_b.at[b], gb_sem.at[b], dev_b(o))
    qkv_scatter.wait()
    for n in range(4):
        gq_ref[:, cols_of(n)] = summed(cols_of(n))
    gk_ref[...] = summed(pl.ds(QCOLS, KVCOLS))
    gv_ref[...] = summed(pl.ds(QCOLS + KVCOLS, KVCOLS))
    for o in ORDER:
        arrived(gain_b.at[plus(b, o)], gb_sem.at[plus(b, o)])
    gain_mine[...] = gain_b[0] + gain_b[1] + gain_b[2] + gain_b[3]
    for i, j in blocks:
        gg_ref[:, at(dp_of(i, j), BLOCK)] = gain_mine[pl.ds(i * 2 + j // 2, 1), cols_of(j % 2)]

    finish(list(unfinished.values()))


def hand_out(*refs):
    for src, dst in zip(refs[:6], refs[6:]):
        dst[...] = src[...]


def local(x_saved, grad_top, query, key, value, segment, w_query, key_weight, value_weight, w_out, gain):
    vmem = pl.BlockSpec(memory_space=pltpu.VMEM)
    hbm = pl.BlockSpec(memory_space=pl.ANY)
    dma = pltpu.SemaphoreType.DMA
    outs = pl.pallas_call(
        kernel,
        out_shape=(
            jax.ShapeDtypeStruct((SUB, WIDTH), BF16),
            jax.ShapeDtypeStruct((BLOCK, QCOLS), BF16),
            jax.ShapeDtypeStruct((BLOCK, KVCOLS), BF16),
            jax.ShapeDtypeStruct((BLOCK, KVCOLS), BF16),
            jax.ShapeDtypeStruct((BLOCK, QCOLS), BF16),
            jax.ShapeDtypeStruct((1, WIDTH), F32),
        ),
        in_specs=[hbm] * 5 + [vmem] * 2 + [hbm] * 4,
        out_specs=(vmem,) * 6,
        scratch_shapes=[
            pltpu.VMEM((2, SUB, WIDTH), BF16),
            pltpu.VMEM((2, TOK, QCOLS), BF16),
            pltpu.VMEM((2, TOK, KVCOLS), BF16),
            pltpu.VMEM((2, TOK, KVCOLS), BF16),
            pltpu.VMEM((2, RING, SUB, GROUP), BF16),
            pltpu.VMEM((2, RING, SUB, GROUP), BF16),
            pltpu.VMEM((2, GROUP, GROUP), BF16),
            pltpu.VMEM((2, GROUP, GROUP), BF16),
            pltpu.VMEM((GROUP, QCOLS), BF16),
            pltpu.VMEM((GROUP, DCOLS), BF16),
            pltpu.VMEM((2, RING, RING, 2, PART, DCOLS), BF16),
            pltpu.VMEM((2, GROUP, QCOLS), BF16),
            pltpu.VMEM((RING, TOK, QCOLS), BF16),
            pltpu.VMEM((2, TOK // 2, QCOLS), BF16),
            pltpu.VMEM((2, TOK, QCOLS), BF16),
            pltpu.VMEM((TOK, QCOLS), BF16),
            pltpu.VMEM((2, 8, TOK, TOK), F32),
            pltpu.VMEM((RING, RING, 2, PART, GROUP), BF16),
            pltpu.VMEM((2, 2, RING, 2, PART // 2, GROUP), BF16),
            pltpu.VMEM((2, 2, RING, 2, PART, GROUP), BF16),
            pltpu.VMEM((2, 2, PART, GROUP), BF16),
            pltpu.VMEM((RING, 2, PART, GROUP), BF16),
            pltpu.VMEM((2, RING, 2, PART, GROUP), BF16),
            pltpu.VMEM((RING, SUB, GROUP), BF16),
            pltpu.VMEM((RING, BLOCK, DCOLS), F32),
            pltpu.VMEM((RING, BLOCK, ALLCOLS), BF16),
            pltpu.VMEM((2, BLOCK // 2, ALLCOLS), BF16),
            pltpu.VMEM((2, BLOCK, ALLCOLS), BF16),
            pltpu.VMEM((2, SUB, HEAD), F32),
            pltpu.VMEM((8, 512), F32),
            pltpu.VMEM((RING, 8, 512), F32),
            pltpu.VMEM((RING, 8, 512), F32),
            pltpu.VMEM((RING, 8, 512), F32),
            dma((400,)),
            dma((2, RING, 2)),
            dma((2, RING, 2, RING, 2)),
            dma((2, RING)),
            dma((2, RING, RING, 2)),
            dma((2, RING, 2)),
            dma((2, 2)),
            dma((2, 2, 2)),
            dma((2, 2, RING, 2)),
            dma((2, RING, 2)),
            dma((2, 2, RING, 2)),
            dma((2, 2, RING, 2, 2)),
            dma((2, 2)),
            dma((2, RING, 2)),
            dma((2,)),
            dma((2, 2)),
            dma((2, 2, 2)),
            dma((RING,)),
            dma((RING,)),
            dma((RING,)),
            dma((9,)),
        ],
        compiler_params=pltpu.CompilerParams(
            collective_id=0, has_side_effects=True, vmem_limit_bytes=63 * 2**20
        ),
        cost_estimate=pl.CostEstimate(flops=23 * 10**9, bytes_accessed=8 * 10**6, transcendentals=10**6),
        name="relay_backward",
    )(
        x_saved[0, 0], grad_top[0, 0], query[0, 0], key[0, 0], value[0, 0], segment[0, 0], gain,
        w_query[0], key_weight[0], value_weight[0], w_out[0],
    )
    bottom, gq, gk, gv, go, gg = pl.pallas_call(
        hand_out,
        out_shape=tuple(jax.ShapeDtypeStruct(out.shape, out.dtype) for out in outs),
        in_specs=[vmem] * 6,
        out_specs=(vmem,) * 6,
        name="hand_out",
    )(*outs)
    return (bottom[None, None], gq[None], gk[None], gv[None], go[None], gg)


def solution(mesh):
    in_specs = (
        P("pipe", "dp", None, "tensor", None),
        P("pipe", "dp", "tensor", None),
        P("pipe", "dp", None, None, "tensor"),
        P("pipe", "dp", None, None, "tensor"),
        P("pipe", "dp", None, None, "tensor"),
        P("pipe", "dp", None, None),
        P("pipe", "dp", "tensor"),
        P("pipe", "dp", "tensor"),
        P("pipe", "dp", "tensor"),
        P("pipe", "dp", "tensor"),
        P("pipe", None),
    )
    out_specs = (
        P("pipe", "dp", "tensor", None),
        P("pipe", "dp", "tensor"),
        P("pipe", "dp", "tensor"),
        P("pipe", "dp", "tensor"),
        P("pipe", "dp", "tensor"),
        P("pipe", None),
    )
    return jax.shard_map(local, mesh=mesh, in_specs=in_specs, out_specs=out_specs, check_vma=False)
```
